256 devices in a mesh: segment: 4 (over y), seq: 64 (over z, x, core).
Axes of the slice: x: 4, y: 4, z: 8, core: 2. Of those that a mesh axis runs over, the one named last changes fastest.
Arguments:
- queries: bfloat16 [4, 8192, 4096], P('segment', 'seq'), as said below
- cache: bfloat16 [4, 2, 32768, 256], P('segment', None, 'seq'), as said below
- packed: bfloat16 [4, 2, 1024, 256], P('segment', None, 'seq'), as said below
- fresh: bfloat16 [4, 8192, 2, 256], P('segment', 'seq'), as said below
- gates: bfloat16 [4, 8192, 96], P('segment', 'seq'), may hold values from -4 to 4
- chosen: int32 [4, 128, 2, 16], P('segment', 'seq'), may hold values from 0 to 511, as said below
Outputs:
- handed: bfloat16 [4, 8192, 4096], P('segment', 'seq')
The draws below stay inside these ranges and needn't reach their ends.
Inputs may be any that keep to these rules, and one draw needn't show every extreme that they name: `chosen`: within one query block and KV head the 16 entries are different blocks of 64 positions. Over both KV heads, at most 2 of the selections of one device's query blocks fall in the cached blocks of one index of seq, and some device reaches 2 for one index of seq within one KV head. `queries`: Real-valued entries. `cache`: Real-valued entries. `packed`: Real-valued entries. `fresh`: Real-valued entries.
All inputs are finite; a program needn't handle non-finite values.
Results may differ from the reference program's by a relative error of at most 0.0045.
Values may be sent and summed in bfloat16 or wider, within the bound.
A program may use at most 128 MiB of HBM per device.

```python
import jax
import jax.numpy as jnp
from jax import lax

HEAD_SIZE = 128
KEY_HEADS = 2
QUERY_PER_KEY = 16
SELECT_SPAN = 64
PICKED_BLOCKS = 16
COMPRESS_STEP = 32
WINDOW_LENGTH = 512
TOKENS_PER_PART = 128
CONTEXT_PER_PART = 512
HQ = 32
TOTAL_TOKENS = 8192
CONTEXT = 32768
CAP = 2
N_SEGMENT = 4
N_SEQ = 64


def draw_queries(key, part):
    key = jax.random.fold_in(key, 5)
    array_shape = (N_SEGMENT, TOKENS_PER_PART * N_SEQ, KEY_HEADS * QUERY_PER_KEY * HEAD_SIZE)
    return (2.5 * jax.random.normal(key, array_shape, jnp.float32)).astype(jnp.bfloat16)


def draw_cache(key, part):
    key = jax.random.fold_in(key, 3)
    array_shape = (N_SEGMENT, KEY_HEADS, CONTEXT_PER_PART * N_SEQ, 2 * HEAD_SIZE)
    return jax.random.normal(key, array_shape, jnp.float32).astype(jnp.bfloat16)


def draw_packed(key, part):
    key = jax.random.fold_in(key, 9)
    array_shape = (N_SEGMENT, KEY_HEADS, CONTEXT_PER_PART * N_SEQ // COMPRESS_STEP, 2 * HEAD_SIZE)
    return jax.random.normal(key, array_shape, jnp.float32).astype(jnp.bfloat16)


def draw_fresh(key, part):
    key = jax.random.fold_in(key, 7)
    array_shape = (N_SEGMENT, TOKENS_PER_PART * N_SEQ, KEY_HEADS, 2 * HEAD_SIZE)
    return jax.random.normal(key, array_shape, jnp.float32).astype(jnp.bfloat16)


def draw_chosen(key, part):
    key = jax.random.fold_in(key, 11)
    blocks_per_part = TOKENS_PER_PART // SELECT_SPAN
    per_partition = blocks_per_part * KEY_HEADS * PICKED_BLOCKS
    per_owner_part = CONTEXT_PER_PART // SELECT_SPAN
    slot_count = N_SEQ * CAP
    count_of_lists = blocks_per_part * KEY_HEADS
    slot_owner = jnp.repeat(jnp.arange(N_SEQ, dtype=jnp.int32), CAP)
    earlier = jnp.tril(jnp.ones((PICKED_BLOCKS, PICKED_BLOCKS), jnp.int32), -1)

    def device_draw(device_key, hot_flags):
        first_owner = jax.random.randint(jax.random.fold_in(device_key, 1), (), 0, N_SEQ)
        shuffle = jax.random.permutation(jax.random.fold_in(device_key, 2), slot_count).astype(jnp.int32)
        priority = shuffle + slot_count * hot_flags[slot_owner] + 2 * slot_count * (slot_owner == first_owner).astype(jnp.int32)
        picked_slots = jnp.argsort(-priority, stable=True)[:per_partition]
        owner_parts = slot_owner[picked_slots].reshape(count_of_lists, PICKED_BLOCKS)
        same_owner = (owner_parts[:, :, None] == owner_parts[:, None, :]).astype(jnp.int32)
        occurrence = jnp.sum(same_owner * earlier[None], axis=2)
        offsets = jax.random.randint(jax.random.fold_in(device_key, 3), (count_of_lists, N_SEQ), 0, per_owner_part)
        base_offset = jnp.take_along_axis(offsets, owner_parts, axis=1)
        block_local = (base_offset + occurrence) % per_owner_part
        return (owner_parts * per_owner_part + block_local).reshape(blocks_per_part, KEY_HEADS, PICKED_BLOCKS)

    def segment_draw(segment_key):
        hot_owners = jax.random.permutation(jax.random.fold_in(segment_key, 4), N_SEQ)[:N_SEQ // 4]
        hot_flags = jnp.zeros((N_SEQ,), jnp.int32).at[hot_owners].set(1)
        device_keys = jax.random.split(jax.random.fold_in(segment_key, 5), N_SEQ)
        final_result = jax.vmap(device_draw, in_axes=(0, None))(device_keys, hot_flags)
        return final_result.reshape(N_SEQ * blocks_per_part, KEY_HEADS, PICKED_BLOCKS)
    segment_keys = jax.random.split(key, N_SEGMENT)
    return jax.vmap(segment_draw)(segment_keys).astype(jnp.int32)


def level_of(rng, shape, shards, least, high):
    loudness = 1.0
    for axis_at, blocks in shards:
        heights = jax.random.uniform(jax.random.fold_in(jax.random.fold_in(rng, 6), axis_at), (blocks,), jnp.float32, least / len(shards), high / len(shards))
        loudness = loudness * jnp.repeat(jnp.exp(heights), shape[axis_at] // blocks).reshape((-1,) + (1,) * (len(shape) - 1 - axis_at))
    return loudness


def centred(own_key, dims, deviation, reach, cuts=(), kind=jnp.bfloat16):
    result = jax.random.normal(own_key, dims, jnp.float32) * deviation
    if len(cuts) > 0:
        result = level_of(own_key, dims, cuts, -0.22, 0.18) * result
    return jnp.clip(result, min=-reach, max=reach).astype(kind)


def setup_inputs(seed: int = 0) -> dict:
    splits = jax.random.split(jax.random.key(seed), 7)
    queries = draw_queries(jax.random.fold_in(splits[6], 71), 0)
    cache = draw_cache(jax.random.fold_in(splits[6], 71), 0)
    packed = draw_packed(jax.random.fold_in(splits[6], 71), 0)
    fresh = draw_fresh(jax.random.fold_in(splits[6], 71), 0)
    gates = centred(splits[4], (N_SEGMENT, TOTAL_TOKENS, 3 * HQ), 1.0, 4.0, ((0, 4), (1, 64)))
    chosen = draw_chosen(jax.random.fold_in(splits[6], 71), 0)
    return {"queries": queries, "cache": cache, "packed": packed, "fresh": fresh, "gates": gates, "chosen": chosen}


score_after_mask = -1.0e30


def attend_branch(query_vector, keys, values, inside, score_form, mix_form):
    scores = jnp.einsum(score_form, query_vector, keys) * (HEAD_SIZE ** -0.5)
    if inside is not None:
        scores = jnp.where(inside, scores, score_after_mask)
    row_peak = jnp.max(scores, axis=-1, keepdims=True)
    rounded = lax.optimization_barrier(jnp.exp(scores - row_peak).astype(jnp.bfloat16))
    weights = rounded.astype(jnp.float32)
    softmax_denominator = jnp.sum(weights, axis=-1)
    softmax_numerator = jnp.einsum(mix_form, weights, values)
    return softmax_numerator / softmax_denominator[..., None]


def segment_output(section_queries, section_cache, segment_packed, section_fresh, section_gates, section_chosen):
    count_of_blocks = CONTEXT // SELECT_SPAN
    cached_block_rows = section_cache.reshape(KEY_HEADS, count_of_blocks, SELECT_SPAN, 2 * HEAD_SIZE)
    summary_keys = segment_packed[..., :HEAD_SIZE].astype(jnp.float32)
    summary_values = segment_packed[..., HEAD_SIZE:].astype(jnp.float32)
    padded_rows = jnp.concatenate([jnp.zeros((WINDOW_LENGTH, KEY_HEADS, 2 * HEAD_SIZE), section_fresh.dtype), section_fresh], axis=0)
    rows_per_head = jnp.arange(KEY_HEADS, dtype=jnp.int32)[:, None]

    def one_block(index_of_block):
        start_position = (index_of_block * SELECT_SPAN).astype(jnp.int32)
        query_vector = lax.dynamic_slice_in_dim(section_queries, start_position, SELECT_SPAN, 0).astype(jnp.float32).reshape(SELECT_SPAN, KEY_HEADS, QUERY_PER_KEY, HEAD_SIZE)
        summary = attend_branch(query_vector, summary_keys, summary_values, None, "tghd,gcd->tghc", "tghc,gcd->tghd")
        picked_key_value = cached_block_rows[rows_per_head, section_chosen[index_of_block]].reshape(KEY_HEADS, PICKED_BLOCKS * SELECT_SPAN, 2 * HEAD_SIZE).astype(jnp.float32)
        picked = attend_branch(query_vector, picked_key_value[..., :HEAD_SIZE], picked_key_value[..., HEAD_SIZE:], None, "tghd,gkd->tghk", "tghk,gkd->tghd")
        near = lax.dynamic_slice_in_dim(padded_rows, start_position, WINDOW_LENGTH + SELECT_SPAN, 0).astype(jnp.float32)
        query_pos = start_position + jnp.arange(SELECT_SPAN, dtype=jnp.int32)
        key_pos = start_position - WINDOW_LENGTH + jnp.arange(WINDOW_LENGTH + SELECT_SPAN, dtype=jnp.int32)
        inside = (key_pos[None, :] <= query_pos[:, None]) & (key_pos[None, :] > query_pos[:, None] - WINDOW_LENGTH) & (key_pos[None, :] >= 0)
        local = attend_branch(query_vector, near[..., :HEAD_SIZE], near[..., HEAD_SIZE:], inside[:, None, None, :], "tghd,kgd->tghk", "tghk,kgd->tghd")
        gate_values = jax.nn.sigmoid(lax.dynamic_slice_in_dim(section_gates, start_position, SELECT_SPAN, 0).astype(jnp.float32)).reshape(SELECT_SPAN, 3, KEY_HEADS, QUERY_PER_KEY, 1)
        combined_output = gate_values[:, 0] * summary + gate_values[:, 1] * picked + gate_values[:, 2] * local
        return combined_output.reshape(SELECT_SPAN, KEY_HEADS * QUERY_PER_KEY * HEAD_SIZE).astype(jnp.bfloat16)

    output_rows = lax.map(one_block, jnp.arange(TOTAL_TOKENS // SELECT_SPAN, dtype=jnp.int32))
    return output_rows.reshape(TOTAL_TOKENS, KEY_HEADS * QUERY_PER_KEY * HEAD_SIZE)


def reference(queries, cache, packed, fresh, gates, chosen):
    attended_output = [segment_output(queries[segment_index], cache[segment_index], packed[segment_index], fresh[segment_index], gates[segment_index], chosen[segment_index]) for segment_index in range(N_SEGMENT)]
    stacked = jnp.stack(attended_output)
    return jnp.roll(stacked, 1, axis=0)
```

```python
import functools

import jax
import jax.numpy as jnp
from jax import lax
from jax.experimental import pallas as pl
from jax.experimental.pallas import tpu as pltpu
from jax.sharding import PartitionSpec as P

HEAD = 128
KV_HEADS = 2
GROUP = 16
SPAN = 64
PICKED = 16
TOKENS = 128
WIDE = KV_HEADS * GROUP * HEAD
Z, X, C = 8, 4, 2
ROW = X * C
PARTS = Z * ROW
SECTIONS = 4
REACH = 4
MESH = pl.DeviceIdType.MESH
MASKED = -1e30
EXP_SCALE = HEAD**-0.5 * 1.4426950408889634


def dot_nt(a, b):
    return lax.dot_general(a, b, (((1,), (1,)), ((), ())), preferred_element_type=jnp.float32)


def dot_nn(a, b):
    return lax.dot_general(a, b, (((1,), (0,)), ((), ())), preferred_element_type=jnp.float32)


def with_ones(v):
    return jnp.concatenate([v, jnp.ones(v.shape, v.dtype)], axis=1)


def request_tile(chosen_row):
    lane = lax.broadcasted_iota(jnp.int32, (128, 128), 1)
    down = lax.broadcasted_iota(jnp.int32, (128, 128), 0)
    across = jnp.broadcast_to(chosen_row, (128, 128))
    column = across.T
    owner_across = lax.shift_right_logical(across, 3)
    owner_down = lax.shift_right_logical(column, 3)
    head_down = lax.shift_right_logical(down, 4) & 1
    code_down = (column & 7) + 8 * head_down
    key_down = down * 16 + code_down
    mine = owner_down == lane
    first = jnp.min(jnp.where(mine, key_down, 1 << 16), axis=0, keepdims=True) & 15
    last = jnp.max(jnp.where(mine, key_down, 0), axis=0, keepdims=True) & 15
    earlier = (owner_down == owner_across) & (down < lane)
    rank = jnp.max(jnp.where(earlier, 1, 0), axis=0, keepdims=True)
    slot = owner_across[0:1] * 2 + rank
    pick = lax.broadcasted_iota(jnp.int32, (8, 128), 0)
    return jnp.where(pick == 0, first, jnp.where(pick == 1, last, slot))


def kernel(
    q_ref, cache_ref, packed_ref, fresh_ref, gates_ref, chosen_ref, out_ref,
    own, r1, r2, r3, l1, l2, l3, x4, stage, slots, pk, fr, qb, gb, tile, tiles, acc, sel, table,
    tile_ss, tile_rs, pk_ss, pk_rs, own_ss, own_rs, misc_ss, misc_rs, q_ss, q_rs,
    ring_ss, ring_rs, pr_ss, pr_rs, x_ss, x_rs, table_sem,
):
    s = lax.axis_index("segment")
    part = lax.axis_index("seq")
    z = lax.div(part, ROW)
    col = lax.rem(part, ROW)
    x = lax.div(col, C)
    c = lax.rem(col, C)
    after = lax.rem(s + 1, SECTIONS)
    before = lax.rem(s + SECTIONS - 1, SECTIONS)

    def in_row(section, d):
        return (section, z * ROW + lax.rem(col + d + ROW, ROW))

    def in_ring(d):
        return (s, lax.rem(z + d + Z, Z) * ROW + col)

    def along(d):
        return (s, lax.rem(part + d + PARTS, PARTS))

    barrier = pltpu.get_barrier_semaphore()
    greeted = (
        [in_row(before, -d) for d in range(ROW)]
        + [in_row(s, d) for d in range(1, ROW)]
        + [in_ring(1), in_ring(-1)]
        + [along(-2), along(-4)]
    )
    for device in greeted:
        pl.semaphore_signal(barrier, inc=1, device_id=device, device_id_type=MESH)
    pl.semaphore_wait(barrier, len(greeted))

    pending = []

    def send(src, dst, send_sem, recv_sem, device):
        copy = pltpu.make_async_remote_copy(
            src_ref=src, dst_ref=dst, send_sem=send_sem, recv_sem=recv_sem,
            device_id=device, device_id_type=MESH,
        )
        copy.start()
        pending.append(copy)

    def arrived(ref, recv_sem):
        pltpu.make_async_remote_copy(
            src_ref=ref, dst_ref=ref, send_sem=recv_sem, recv_sem=recv_sem,
            device_id=in_ring(1), device_id_type=MESH,
        ).wait_recv()

    def half(ref, h):
        return ref.at[pl.ds(8 * h, 8)]

    straight = (after, part)
    for d in range(X):
        to_x = lax.rem(x + d, X)
        send(packed_ref, pk.at[:, c, z, x], pk_ss.at[d], pk_rs.at[x], (after, z * ROW + to_x * C + c))
    for h in range(2):
        send(half(cache_ref, h), half(own, h), own_ss.at[h], own_rs.at[h], straight)
    tile[...] = request_tile(chosen_ref[...])
    for d in range(ROW):
        send(tile, tiles.at[col], tile_ss.at[d], tile_rs.at[col], in_row(after, d))
    send(fresh_ref, fr.at[REACH], misc_ss.at[0], misc_rs.at[0], straight)
    send(gates_ref, gb, misc_ss.at[1], misc_rs.at[1], straight)

    def send_queries(i):
        send(q_ref.at[:, pl.ds(1024 * i, 1024)], qb.at[i], q_ss.at[i], q_rs.at[i], straight)

    right = [own, r1, r2, r3, x4]
    left = [own, l1, l2, l3, x4]

    def ring_send(k, h):
        if k < 4 or h == 0:
            send(half(right[k - 1], h), half(right[k], h), ring_ss.at[0, k - 1, h], ring_rs.at[0, k - 1, h], in_ring(1))
        if k < 4 or h == 1:
            send(half(left[k - 1], h), half(left[k], h), ring_ss.at[1, k - 1, h], ring_rs.at[1, k - 1, h], in_ring(-1))

    def ring_arrived(k, h):
        if k < 4 or h == 0:
            arrived(half(right[k], h), ring_rs.at[0, k - 1, h])
        if k < 4 or h == 1:
            arrived(half(left[k], h), ring_rs.at[1, k - 1, h])

    def packed_at(d, whole, g):
        at = lax.rem(z + d + Z, Z)
        return pk.at[:, c, at] if whole else pk.at[g, c, at]

    def packed_send(k):
        for way, sign in ((0, 1), (1, -1)):
            ref = packed_at(-sign * (k - 1), k < 4, way)
            send(ref, ref, pr_ss.at[way, k - 1], pr_rs.at[way, k - 1], in_ring(sign))

    def packed_arrived(k):
        for way, sign in ((0, 1), (1, -1)):
            arrived(packed_at(-sign * k, k < 4, way), pr_rs.at[way, k - 1])

    def serve(step, shard, d):
        owner = lax.rem(z + d + Z, Z) * ROW + col
        for e in range(ROW):
            peer = lax.rem(col + e, ROW)
            for r in range(2):
                block = shard[table[peer, r, owner]]
                if e == 0:
                    slots[owner, r] = block
                else:
                    stage[step, e - 1, r] = block
            if e > 0:
                send(stage.at[step, e - 1], slots.at[owner], x_ss.at[step, e], x_rs.at[step, e], in_row(s, e))

    def served(step, d):
        at = lax.rem(z + d + Z, Z)
        for e in range(1, ROW):
            peer = lax.rem(col - e + ROW, ROW)
            arrived(slots.at[at * ROW + peer], x_rs.at[step, e])

    def gate(branch, head, rows):
        logits = gb[rows, :].astype(jnp.float32)
        lane = lax.broadcasted_iota(jnp.int32, logits.shape, 1)
        picked = jnp.sum(jnp.where(lane == branch * 32 + head, logits, 0.0), axis=1, keepdims=True)
        return 1.0 / (1.0 + jnp.exp(-picked))

    def early_unit(i, u):
        g = i // 2
        q = jnp.concatenate(
            [qb[i, :, pl.ds(pl.multiple_of((2 * u + m) * HEAD, HEAD), HEAD)] for m in range(2)], axis=0
        )
        kv = pk[g].reshape(C * Z * X * 16, 2 * HEAD)
        scores = dot_nt(q, kv[:, :HEAD])
        peak = jnp.max(scores, axis=1, keepdims=True)
        weights = jnp.exp2((scores - peak) * EXP_SCALE).astype(jnp.bfloat16)
        mixed = dot_nn(weights, with_ones(kv[:, HEAD:]))
        summary = mixed[:, :HEAD] / mixed[:, HEAD:]

        near = fr[:, :, pl.ds(g * 2 * HEAD, 2 * HEAD)].reshape((REACH + 1) * TOKENS, 2 * HEAD)
        scores = dot_nt(q, near[:, :HEAD])
        key = lax.broadcasted_iota(jnp.int32, (2 * TOKENS, TOKENS), 1)
        token = lax.broadcasted_iota(jnp.int32, (2 * TOKENS, TOKENS), 0) & (TOKENS - 1)
        beyond = key > token
        piece = [scores[:, TOKENS * n : TOKENS * (n + 1)] for n in range(REACH + 1)]
        for n in range(REACH):
            piece[n] = jnp.where(key >= (REACH - n - part) * 1024, piece[n], MASKED)
        piece[0] = jnp.where(beyond, piece[0], piece[REACH])
        joined = jnp.concatenate(piece[:REACH], axis=1)
        peak = jnp.max(joined, axis=1, keepdims=True)
        weights = jnp.exp2((joined - peak) * EXP_SCALE)
        first = weights[:, :TOKENS]
        weights = jnp.concatenate(
            [jnp.where(beyond, first, 0.0), weights[:, TOKENS:], jnp.where(beyond, 0.0, first)], axis=1
        ).astype(jnp.bfloat16)
        mixed = dot_nn(weights, with_ones(near[:, HEAD:]))
        local = mixed[:, :HEAD] / mixed[:, HEAD:]

        for m in range(2):
            head = 8 * i + 2 * u + m
            rows = slice(TOKENS * m, TOKENS * (m + 1))
            everyone = slice(0, TOKENS)
            acc[8 * i + 2 * u + m] = (
                gate(0, head, everyone) * summary[rows] + gate(2, head, everyone) * local[rows]
            )

    def early(i):
        def body(u, carry):
            early_unit(i, u)
            return carry

        lax.fori_loop(0, 4, body, 0)

    def late_unit(b, g, u):
        rows = slice(SPAN * b, SPAN * (b + 1))
        heads = [16 * g + 4 * u + m for m in range(4)]
        q = jnp.concatenate(
            [qb[h // 8, rows, (h % 8) * HEAD : (h % 8 + 1) * HEAD] for h in heads], axis=0
        )
        kv = sel[2 * b + g]
        scores = dot_nt(q, kv[:, :HEAD])
        peak = jnp.max(scores, axis=1, keepdims=True)
        weights = jnp.exp2((scores - peak) * EXP_SCALE).astype(jnp.bfloat16)
        mixed = dot_nn(weights, with_ones(kv[:, HEAD:]))
        picked = mixed[:, :HEAD] / mixed[:, HEAD:]
        for m, h in enumerate(heads):
            one = picked[SPAN * m : SPAN * (m + 1)]
            out_ref[rows, h * HEAD : (h + 1) * HEAD] = (
                acc[h, rows, :] + gate(1, h, rows) * one
            ).astype(jnp.bfloat16)

    for d in range(X):
        arrived(pk.at[:, c, z, d], pk_rs.at[d])
    packed_send(1)
    arrived(half(own, 0), own_rs.at[0])
    ring_send(1, 0)
    packed_arrived(1)
    packed_send(2)
    arrived(half(own, 1), own_rs.at[1])
    ring_send(1, 1)
    send_queries(0)
    send_queries(1)
    for d in range(ROW):
        arrived(tiles.at[d], tile_rs.at[d])
    to_scalar = pltpu.make_async_copy(tiles, table, table_sem)
    to_scalar.start()
    to_scalar.wait()
    serve(0, own, 0)
    packed_arrived(2)
    packed_send(3)
    arrived(fr.at[REACH], misc_rs.at[0])
    send(fr.at[REACH], fr.at[2], misc_ss.at[2], misc_rs.at[2], along(2))
    send(fr.at[REACH], fr.at[0], misc_ss.at[3], misc_rs.at[3], along(4))
    ring_arrived(1, 0)
    ring_send(2, 0)
    packed_arrived(3)
    packed_send(4)
    send_queries(2)
    send_queries(3)
    ring_arrived(1, 1)
    ring_send(2, 1)
    serve(1, r1, -1)
    serve(2, l1, 1)
    packed_arrived(4)
    sibling = (s, part + 1 - 2 * c)
    send(pk.at[:, c], pk.at[:, c], misc_ss.at[4], misc_rs.at[4], sibling)
    arrived(fr.at[2], misc_rs.at[2])
    arrived(fr.at[0], misc_rs.at[3])
    send(fr.at[4 - 2 * c], fr.at[3], misc_ss.at[5], misc_rs.at[5], sibling)
    send(fr.at[2 - 2 * c], fr.at[1], misc_ss.at[6], misc_rs.at[6], sibling)
    ring_arrived(2, 0)
    ring_send(3, 0)
    arrived(pk.at[:, 1 - c], misc_rs.at[4])
    arrived(fr.at[3], misc_rs.at[5])
    arrived(fr.at[1], misc_rs.at[6])
    arrived(gb, misc_rs.at[1])
    arrived(qb.at[0], q_rs.at[0])
    early(0)
    ring_arrived(2, 1)
    ring_send(3, 1)
    serve(3, r2, -2)
    serve(4, l2, 2)
    arrived(qb.at[1], q_rs.at[1])
    early(1)
    ring_arrived(3, 0)
    ring_send(4, 0)
    arrived(qb.at[2], q_rs.at[2])
    early(2)
    ring_arrived(3, 1)
    ring_send(4, 1)
    serve(5, r3, -3)
    serve(6, l3, 3)
    arrived(qb.at[3], q_rs.at[3])
    early(3)
    ring_arrived(4, 0)
    ring_arrived(4, 1)
    serve(7, x4, 4)
    for step, d in enumerate((0, -1, 1, -2, 2, -3, 3, 4)):
        served(step, d)
    for e in range(KV_HEADS * 2 * PICKED):
        spot = table[col, 2, e]
        sel[e // PICKED, pl.ds((e % PICKED) * SPAN, SPAN), :] = slots[lax.div(spot, 2), lax.rem(spot, 2)]
    for b in range(2):
        for g in range(KV_HEADS):
            for u in range(4):
                late_unit(b, g, u)
    for copy in pending:
        copy.wait_send()


def per_device(queries, cache, packed, fresh, gates, chosen):
    q = queries[0]
    blocks = cache[0].reshape(KV_HEADS * 8, SPAN, 2 * HEAD)
    near = fresh[0].reshape(TOKENS, KV_HEADS * 2 * HEAD)
    wanted = jnp.pad(chosen[0].reshape(1, 64), ((0, 0), (0, 64)), constant_values=1 << 12)
    bf16, dma = jnp.bfloat16, pltpu.SemaphoreType.DMA
    shard = pltpu.VMEM((16, SPAN, 2 * HEAD), bf16)
    anywhere = pl.BlockSpec(memory_space=pl.ANY)
    vmem = pl.BlockSpec(memory_space=pltpu.VMEM)
    out = pl.pallas_call(
        kernel,
        out_shape=jax.ShapeDtypeStruct((TOKENS, WIDE), bf16),
        in_specs=[anywhere, anywhere, anywhere, anywhere, anywhere, vmem],
        out_specs=vmem,
        scratch_shapes=[shard] * 8
        + [
            pltpu.VMEM((8, ROW - 1, 2, SPAN, 2 * HEAD), bf16),
            pltpu.VMEM((PARTS, 2, SPAN, 2 * HEAD), bf16),
            pltpu.VMEM((KV_HEADS, C, Z, X, 16, 2 * HEAD), bf16),
            pltpu.VMEM((REACH + 1, TOKENS, KV_HEADS * 2 * HEAD), bf16),
            pltpu.VMEM((4, TOKENS, 1024), bf16),
            pltpu.VMEM((TOKENS, 96), bf16),
            pltpu.VMEM((8, 128), jnp.int32),
            pltpu.VMEM((ROW, 8, 128), jnp.int32),
            pltpu.VMEM((32, TOKENS, HEAD), jnp.float32),
            pltpu.VMEM((4, PICKED * SPAN, 2 * HEAD), bf16),
            pltpu.SMEM((ROW, 8, 128), jnp.int32),
            dma((ROW,)), dma((ROW,)),
            dma((X,)), dma((X,)),
            dma((2,)), dma((2,)),
            dma((7,)), dma((7,)),
            dma((4,)), dma((4,)),
            dma((2, 4, 2)), dma((2, 4, 2)),
            dma((2, 4)), dma((2, 4)),
            dma((8, ROW)), dma((8, ROW)),
            dma,
        ],
        compiler_params=pltpu.CompilerParams(
            collective_id=1, has_side_effects=True, vmem_limit_bytes=56 * 2**20
        ),
    )(q, blocks, packed[0], near, gates[0], wanted)
    return out[None]


def solution(mesh):
    placed = (
        P("segment", "seq", None),
        P("segment", None, "seq", None),
        P("segment", None, "seq", None),
        P("segment", "seq", None, None),
        P("segment", "seq", None),
        P("segment", "seq", None, None),
    )
    return jax.shard_map(
        per_device, mesh=mesh, in_specs=placed, out_specs=P("segment", "seq", None), check_vma=False
    )
```

```python
import functools

import jax
import jax.numpy as jnp
from jax import lax
from jax.experimental import pallas as pl
from jax.experimental.pallas import tpu as pltpu
from jax.sharding import PartitionSpec as P

HEAD = 128
KV_HEADS = 2
GROUP = 16
SPAN = 64
PICKED = 16
TOKENS = 128
WIDE = KV_HEADS * GROUP * HEAD
Z, X, C = 8, 4, 2
ROW = X * C
PARTS = Z * ROW
SECTIONS = 4
REACH = 4
CHUNKS = 4
PIECE = KV_HEADS * 8 // CHUNKS
MESH = pl.DeviceIdType.MESH
MASKED = -1e30
EXP_SCALE = HEAD**-0.5 * 1.4426950408889634


def dot_nt(a, b):
    return lax.dot_general(a, b, (((1,), (1,)), ((), ())), preferred_element_type=jnp.float32)


def dot_nn(a, b):
    return lax.dot_general(a, b, (((1,), (0,)), ((), ())), preferred_element_type=jnp.float32)


def with_ones(v):
    return jnp.concatenate([v, jnp.ones(v.shape, v.dtype)], axis=1)


def request_tile(chosen_row):
    lane = lax.broadcasted_iota(jnp.int32, (128, 128), 1)
    down = lax.broadcasted_iota(jnp.int32, (128, 128), 0)
    across = jnp.broadcast_to(chosen_row, (128, 128))
    column = across.T
    owner_across = lax.shift_right_logical(across, 3)
    owner_down = lax.shift_right_logical(column, 3)
    head_down = lax.shift_right_logical(down, 4) & 1
    code_down = (column & 7) + 8 * head_down
    key_down = down * 16 + code_down
    mine = owner_down == lane
    first = jnp.min(jnp.where(mine, key_down, 1 << 16), axis=0, keepdims=True) & 15
    last = jnp.max(jnp.where(mine, key_down, 0), axis=0, keepdims=True) & 15
    earlier = (owner_down == owner_across) & (down < lane)
    rank = jnp.max(jnp.where(earlier, 1, 0), axis=0, keepdims=True)
    slot = owner_across[0:1] * 2 + rank
    pick = lax.broadcasted_iota(jnp.int32, (8, 128), 0)
    return jnp.where(pick == 0, first, jnp.where(pick == 1, last, slot))


def chosen_row(chosen_ref, listed):
    listed[...] = jnp.zeros(listed.shape, listed.dtype)
    for b in range(2):
        listed[KV_HEADS * b : KV_HEADS * (b + 1), 0:PICKED] = chosen_ref[b]
    lane = lax.broadcasted_iota(jnp.int32, (1, 128), 1)
    row = jnp.full((1, 128), 1 << 12, jnp.int32)
    for i in range(2 * KV_HEADS):
        part = listed[i : i + 1, :]
        if i > 0:
            part = pltpu.roll(part, PICKED * i, 1)
        row = jnp.where((lane >= PICKED * i) & (lane < PICKED * (i + 1)), part, row)
    return row


def kernel(
    q_ref, cache_ref, packed_ref, fresh_ref, gates_ref, chosen_ref, out_ref,
    own, r1, r2, r3, l1, l2, l3, x4, stage, slots, pk, raw, behind, fr, qb, gb, gate_of,
    listed, tile, tiles, acc, sel, table,
    tile_ss, tile_rs, pk_ss, pk_rs, own_ss, own_rs, misc_ss, misc_rs, q_ss, q_rs,
    ring_ss, ring_rs, pr_ss, pr_rs, x_ss, x_rs, local_sem,
):
    s = lax.axis_index("segment")
    part = lax.axis_index("seq")
    z = lax.div(part, ROW)
    col = lax.rem(part, ROW)
    x = lax.div(col, C)
    c = lax.rem(col, C)
    after = lax.rem(s + 1, SECTIONS)
    before = lax.rem(s + SECTIONS - 1, SECTIONS)

    def in_row(section, d):
        return (section, z * ROW + lax.rem(col + d + ROW, ROW))

    def in_ring(d):
        return (s, lax.rem(z + d + Z, Z) * ROW + col)

    def along(d):
        return (s, lax.rem(part + d + PARTS, PARTS))

    barrier = pltpu.get_barrier_semaphore()
    greeted = (
        [in_row(before, -d) for d in range(ROW)]
        + [in_row(s, d) for d in range(1, ROW)]
        + [in_ring(1), in_ring(-1)]
        + [along(-2), along(-4)]
    )
    for device in greeted:
        pl.semaphore_signal(barrier, inc=1, device_id=device, device_id_type=MESH)
    pl.semaphore_wait(barrier, len(greeted))

    pending = []

    def send(src, dst, send_sem, recv_sem, device):
        copy = pltpu.make_async_remote_copy(
            src_ref=src, dst_ref=dst, send_sem=send_sem, recv_sem=recv_sem,
            device_id=device, device_id_type=MESH,
        )
        copy.start()
        pending.append(copy)

    others = ((1, 0), (3, 0), (1, 1), (3, 1), (2, 0), (2, 1), (0, 1))

    def there(dx, dc):
        return lax.rem(x + dx + X, X) * C + lax.rem(c + dc, C)

    def arrived(ref, recv_sem):
        pltpu.make_async_remote_copy(
            src_ref=ref, dst_ref=ref, send_sem=recv_sem, recv_sem=recv_sem,
            device_id=in_ring(1), device_id_type=MESH,
        ).wait_recv()

    def piece_of(ref, i):
        return ref.at[pl.ds(PIECE * i, PIECE)]

    straight = (after, part)

    def send_cache(i):
        send(piece_of(cache_ref, i), piece_of(own, i), own_ss.at[i], own_rs.at[i], straight)

    def send_queries(i):
        send(q_ref.at[:, pl.ds(1024 * i, 1024)], qb.at[i], q_ss.at[i], q_rs.at[i], straight)

    def ring_send(k, i):
        for way, (held, sign) in enumerate(((right, 1), (left, -1))):
            if k < 4 or i // (CHUNKS // 2) == way:
                send(
                    piece_of(held[k - 1], i), piece_of(held[k], i),
                    ring_ss.at[way, k - 1, i], ring_rs.at[way, k - 1, i], in_ring(sign),
                )

    def ring_arrived(k, i):
        for way, held in enumerate((right, left)):
            if k < 4 or i // (CHUNKS // 2) == way:
                arrived(piece_of(held[k], i), ring_rs.at[way, k - 1, i])

    right = [own, r1, r2, r3, x4]
    left = [own, l1, l2, l3, x4]

    def packed_at(d, whole, g):
        at = lax.rem(z + d + Z, Z)
        return pk.at[:, c, at] if whole else pk.at[g, c, at]

    def packed_send(k):
        for way, sign in ((0, 1), (1, -1)):
            ref = packed_at(-sign * (k - 1), k < 4, way)
            send(ref, ref, pr_ss.at[way, k - 1], pr_rs.at[way, k - 1], in_ring(sign))

    def packed_arrived(k):
        for way, sign in ((0, 1), (1, -1)):
            arrived(packed_at(-sign * k, k < 4, way), pr_rs.at[way, k - 1])

    def serve(step, shard, d):
        owner = lax.rem(z + d + Z, Z) * ROW + col
        for e, (dx, dc) in enumerate(others + ((0, 0),)):
            peer = there(dx, dc)
            for r in range(2):
                block = shard[table[peer, r, owner]]
                if e == ROW - 1:
                    slots[owner, r] = block
                else:
                    stage[step, e, r] = block
            if e < ROW - 1:
                send(stage.at[step, e], slots.at[owner], x_ss.at[step, e], x_rs.at[step, e], (s, z * ROW + peer))

    def served(step, d):
        at = lax.rem(z + d + Z, Z)
        for e, (dx, dc) in enumerate(others):
            arrived(slots.at[at * ROW + there(-dx, dc)], x_rs.at[step, e])

    def gate(branch, head, rows):
        values = gate_of[rows, :]
        lane = lax.broadcasted_iota(jnp.int32, values.shape, 1)
        return jnp.sum(jnp.where(lane == branch * 32 + head, values, 0.0), axis=1, keepdims=True)

    def early_unit(i, u):
        g = i // 2
        q = jnp.concatenate(
            [qb[i, :, pl.ds(pl.multiple_of((2 * u + m) * HEAD, HEAD), HEAD)] for m in range(2)], axis=0
        )
        kv = pk[g].reshape(C * Z * X * 16, 2 * HEAD)
        scores = dot_nt(q, kv[:, :HEAD])
        peak = jnp.max(scores, axis=1, keepdims=True)
        weights = jnp.exp2((scores - peak) * EXP_SCALE).astype(jnp.bfloat16)
        mixed = dot_nn(weights, with_ones(kv[:, HEAD:]))
        summary = mixed[:, :HEAD] / mixed[:, HEAD:]

        near = fr[:, :, pl.ds(g * 2 * HEAD, 2 * HEAD)].reshape((REACH + 1) * TOKENS, 2 * HEAD)
        scores = dot_nt(q, near[:, :HEAD])
        key = lax.broadcasted_iota(jnp.int32, (2 * TOKENS, TOKENS), 1)
        token = lax.broadcasted_iota(jnp.int32, (2 * TOKENS, TOKENS), 0) & (TOKENS - 1)
        beyond = key > token
        piece = [scores[:, TOKENS * n : TOKENS * (n + 1)] for n in range(REACH + 1)]
        for n in range(REACH):
            piece[n] = jnp.where(key >= (REACH - n - part) * 1024, piece[n], MASKED)
        piece[0] = jnp.where(beyond, piece[0], piece[REACH])
        joined = jnp.concatenate(piece[:REACH], axis=1)
        peak = jnp.max(joined, axis=1, keepdims=True)
        weights = jnp.exp2((joined - peak) * EXP_SCALE)
        first = weights[:, :TOKENS]
        weights = jnp.concatenate(
            [jnp.where(beyond, first, 0.0), weights[:, TOKENS:], jnp.where(beyond, 0.0, first)], axis=1
        ).astype(jnp.bfloat16)
        mixed = dot_nn(weights, with_ones(near[:, HEAD:]))
        local = mixed[:, :HEAD] / mixed[:, HEAD:]

        for m in range(2):
            head = 8 * i + 2 * u + m
            rows = slice(TOKENS * m, TOKENS * (m + 1))
            everyone = slice(0, TOKENS)
            acc[8 * i + 2 * u + m] = (
                gate(0, head, everyone) * summary[rows] + gate(2, head, everyone) * local[rows]
            )

    def early(i, half):
        def body(u, carry):
            early_unit(i, u)
            return carry

        lax.fori_loop(2 * half, 2 * half + 2, body, 0)

    def late_unit(b, g, u):
        rows = slice(SPAN * b, SPAN * (b + 1))
        heads = [16 * g + 4 * u + m for m in range(4)]
        q = jnp.concatenate(
            [qb[h // 8, rows, (h % 8) * HEAD : (h % 8 + 1) * HEAD] for h in heads], axis=0
        )
        kv = sel[2 * b + g]
        scores = dot_nt(q, kv[:, :HEAD])
        peak = jnp.max(scores, axis=1, keepdims=True)
        weights = jnp.exp2((scores - peak) * EXP_SCALE).astype(jnp.bfloat16)
        mixed = dot_nn(weights, with_ones(kv[:, HEAD:]))
        picked = mixed[:, :HEAD] / mixed[:, HEAD:]
        for m, h in enumerate(heads):
            one = picked[SPAN * m : SPAN * (m + 1)]
            out_ref[rows, h * HEAD : (h + 1) * HEAD] = (
                acc[h, rows, :] + gate(1, h, rows) * one
            ).astype(jnp.bfloat16)

    send_cache(0)
    for d in range(X):
        to_x = lax.rem(x + d, X)
        send(packed_ref, pk.at[:, c, z, x], pk_ss.at[d], pk_rs.at[x], (after, z * ROW + to_x * C + c))
    send_cache(1)
    fetch = pltpu.make_async_copy(fresh_ref, raw, local_sem.at[0])
    fetch.start()
    tile[...] = request_tile(chosen_row(chosen_ref, listed))
    for d in range(ROW):
        send(tile, tiles.at[col], tile_ss.at[d], tile_rs.at[col], in_row(after, d))
    send(gates_ref, gb, misc_ss.at[1], misc_rs.at[1], straight)
    fetch.wait()
    for g in range(KV_HEADS):
        behind[0, :, 2 * HEAD * g : 2 * HEAD * (g + 1)] = raw[:, g, :]
    send(behind.at[0], behind.at[1], misc_ss.at[2], misc_rs.at[2], along(2))
    send(behind.at[0], behind.at[2], misc_ss.at[3], misc_rs.at[3], along(4))
    sibling = (s, part + 1 - 2 * c)

    for i in range(CHUNKS):
        arrived(piece_of(own, i), own_rs.at[i])
        ring_send(1, i)
        if i + 2 < CHUNKS:
            send_cache(i + 2)
        if i == 0:
            for d in range(X):
                arrived(pk.at[:, c, z, d], pk_rs.at[d])
            packed_send(1)
        if i == 2:
            packed_arrived(1)
            packed_send(2)
    for d in range(ROW):
        arrived(tiles.at[d], tile_rs.at[d])
    to_scalar = pltpu.make_async_copy(tiles, table, local_sem.at[1])
    to_scalar.start()
    to_scalar.wait()
    serve(0, own, 0)
    arrived(behind.at[1], misc_rs.at[2])
    arrived(behind.at[2], misc_rs.at[3])
    for n, spot in enumerate((4, 2, 0)):
        send(behind.at[n], fr.at[spot], misc_ss.at[7 + n], misc_rs.at[7 + n], straight)
    for i in range(CHUNKS):
        ring_arrived(1, i)
        ring_send(2, i)
        if i == 0:
            packed_arrived(2)
            packed_send(3)
        if i == 2:
            packed_arrived(3)
            packed_send(4)
    send_queries(0)
    send_queries(1)
    serve(1, r1, -1)
    serve(2, l1, 1)
    for i in range(CHUNKS):
        ring_arrived(2, i)
        ring_send(3, i)
        if i == 0:
            packed_arrived(4)
            send(pk.at[:, c], pk.at[:, c], misc_ss.at[4], misc_rs.at[4], sibling)
        if i == 1:
            for n, spot in enumerate((4, 2, 0)):
                arrived(fr.at[spot], misc_rs.at[7 + n])
            send(fr.at[4 - 2 * c], fr.at[3], misc_ss.at[5], misc_rs.at[5], sibling)
            send(fr.at[2 - 2 * c], fr.at[1], misc_ss.at[6], misc_rs.at[6], sibling)
    serve(3, r2, -2)
    serve(4, l2, 2)
    arrived(gb, misc_rs.at[1])
    logits = jnp.concatenate([gb[...].astype(jnp.float32), jnp.zeros((32, TOKENS), jnp.float32)], axis=0)
    gate_of[...] = 1.0 / (1.0 + jnp.exp(-logits.T))
    arrived(pk.at[:, 1 - c], misc_rs.at[4])
    arrived(fr.at[3], misc_rs.at[5])
    arrived(fr.at[1], misc_rs.at[6])
    arrived(qb.at[0], q_rs.at[0])
    send_queries(2)
    for i in range(CHUNKS):
        ring_arrived(3, i)
        ring_send(4, i)
        if i == 2:
            arrived(qb.at[1], q_rs.at[1])
            send_queries(3)
        if i < 3:
            early(i // 2, i % 2)
    serve(5, r3, -3)
    serve(6, l3, 3)
    early(1, 1)
    for i in range(CHUNKS):
        ring_arrived(4, i)
    serve(7, x4, 4)
    for i in (2, 3):
        arrived(qb.at[i], q_rs.at[i])
        early(i, 0)
        early(i, 1)
    for step, d in enumerate((0, -1, 1, -2, 2, -3, 3, 4)):
        served(step, d)
    for e in range(KV_HEADS * 2 * PICKED):
        spot = table[col, 2, e]
        sel[e // PICKED, pl.ds((e % PICKED) * SPAN, SPAN), :] = slots[lax.div(spot, 2), lax.rem(spot, 2)]
    for b in range(2):
        for g in range(KV_HEADS):
            for u in range(4):
                late_unit(b, g, u)
    for copy in pending:
        copy.wait_send()


def per_device(queries, cache, packed, fresh, gates, chosen):
    blocks = cache[0].reshape(KV_HEADS * 8, SPAN, 2 * HEAD)
    bf16, dma = jnp.bfloat16, pltpu.SemaphoreType.DMA
    shard = pltpu.VMEM((16, SPAN, 2 * HEAD), bf16)
    anywhere = pl.BlockSpec(memory_space=pltpu.HBM)
    vmem = pl.BlockSpec(memory_space=pltpu.VMEM)
    out = pl.pallas_call(
        kernel,
        out_shape=jax.ShapeDtypeStruct((TOKENS, WIDE), bf16),
        in_specs=[anywhere, anywhere, anywhere, anywhere, anywhere, vmem],
        out_specs=vmem,
        scratch_shapes=[shard] * 8
        + [
            pltpu.VMEM((8, ROW - 1, 2, SPAN, 2 * HEAD), bf16),
            pltpu.VMEM((PARTS, 2, SPAN, 2 * HEAD), bf16),
            pltpu.VMEM((KV_HEADS, C, Z, X, 16, 2 * HEAD), bf16),
            pltpu.VMEM((TOKENS, KV_HEADS, 2 * HEAD), bf16),
            pltpu.VMEM((3, TOKENS, KV_HEADS * 2 * HEAD), bf16),
            pltpu.VMEM((REACH + 1, TOKENS, KV_HEADS * 2 * HEAD), bf16),
            pltpu.VMEM((4, TOKENS, 1024), bf16),
            pltpu.VMEM((96, TOKENS), bf16),
            pltpu.VMEM((TOKENS, 128), jnp.float32),
            pltpu.VMEM((8, 128), jnp.int32),
            pltpu.VMEM((8, 128), jnp.int32),
            pltpu.VMEM((ROW, 8, 128), jnp.int32),
            pltpu.VMEM((32, TOKENS, HEAD), jnp.float32),
            pltpu.VMEM((4, PICKED * SPAN, 2 * HEAD), bf16),
            pltpu.SMEM((ROW, 8, 128), jnp.int32),
            dma((ROW,)), dma((ROW,)),
            dma((X,)), dma((X,)),
            dma((CHUNKS,)), dma((CHUNKS,)),
            dma((10,)), dma((10,)),
            dma((4,)), dma((4,)),
            dma((2, 4, CHUNKS)), dma((2, 4, CHUNKS)),
            dma((2, 4)), dma((2, 4)),
            dma((8, ROW)), dma((8, ROW)),
            dma((2,)),
        ],
        compiler_params=pltpu.CompilerParams(
            collective_id=1, has_side_effects=True, vmem_limit_bytes=56 * 2**20
        ),
    )(queries[0], blocks, packed[0], fresh[0], gates[0].T, chosen[0])
    return out[None]


def solution(mesh):
    placed = (
        P("segment", "seq", None),
        P("segment", None, "seq", None),
        P("segment", None, "seq", None),
        P("segment", "seq", None, None),
        P("segment", "seq", None),
        P("segment", "seq", None, None),
    )
    return jax.shard_map(
        per_device, mesh=mesh, in_specs=placed, out_specs=P("segment", "seq", None), check_vma=False
    )
```

```python
import functools

import jax
import jax.numpy as jnp
from jax import lax
from jax.experimental import pallas as pl
from jax.experimental.pallas import tpu as pltpu
from jax.sharding import PartitionSpec as P

HEAD = 128
KV_HEADS = 2
GROUP = 16
SPAN = 64
PICKED = 16
TOKENS = 128
WIDE = KV_HEADS * GROUP * HEAD
Z, X, C = 8, 4, 2
ROW = X * C
PARTS = Z * ROW
SECTIONS = 4
REACH = 4
CHUNKS = 4
PIECE = KV_HEADS * 8 // CHUNKS
MESH = pl.DeviceIdType.MESH
MASKED = -1e30
EXP_SCALE = HEAD**-0.5 * 1.4426950408889634


def dot_nt(a, b):
    return lax.dot_general(a, b, (((1,), (1,)), ((), ())), preferred_element_type=jnp.float32)


def dot_nn(a, b):
    return lax.dot_general(a, b, (((1,), (0,)), ((), ())), preferred_element_type=jnp.float32)


def with_ones(v):
    return jnp.concatenate([v, jnp.ones(v.shape, v.dtype)], axis=1)


def request_tile(chosen_row):
    lane = lax.broadcasted_iota(jnp.int32, (128, 128), 1)
    down = lax.broadcasted_iota(jnp.int32, (128, 128), 0)
    across = jnp.broadcast_to(chosen_row, (128, 128))
    column = across.T
    owner_across = lax.shift_right_logical(across, 3)
    owner_down = lax.shift_right_logical(column, 3)
    head_down = lax.shift_right_logical(down, 4) & 1
    code_down = (column & 7) + 8 * head_down
    key_down = down * 16 + code_down
    mine = owner_down == lane
    first = jnp.min(jnp.where(mine, key_down, 1 << 16), axis=0, keepdims=True) & 15
    last = jnp.max(jnp.where(mine, key_down, 0), axis=0, keepdims=True) & 15
    earlier = (owner_down == owner_across) & (down < lane)
    rank = jnp.max(jnp.where(earlier, 1, 0), axis=0, keepdims=True)
    slot = owner_across[0:1] * 2 + rank
    pick = lax.broadcasted_iota(jnp.int32, (8, 128), 0)
    return jnp.where(pick == 0, first, jnp.where(pick == 1, last, slot))


def chosen_row(chosen_ref, listed):
    listed[...] = jnp.zeros(listed.shape, listed.dtype)
    for b in range(2):
        listed[KV_HEADS * b : KV_HEADS * (b + 1), 0:PICKED] = chosen_ref[b]
    lane = lax.broadcasted_iota(jnp.int32, (1, 128), 1)
    row = jnp.full((1, 128), 1 << 12, jnp.int32)
    for i in range(2 * KV_HEADS):
        part = listed[i : i + 1, :]
        if i > 0:
            part = pltpu.roll(part, PICKED * i, 1)
        row = jnp.where((lane >= PICKED * i) & (lane < PICKED * (i + 1)), part, row)
    return row


def kernel(
    q_ref, cache_ref, packed_ref, fresh_ref, gates_ref, chosen_ref, out_ref,
    own, r1, r2, r3, l1, l2, l3, x4, stage, slots, home_pk, pk, raw, behind, fr, qb, gb,
    gate_of, chosen, listed, tile, tiles, acc, sel, table,
    tile_ss, tile_rs, pk_ss, pk_rs, own_ss, own_rs, misc_ss, misc_rs, q_ss, q_rs,
    ring_ss, ring_rs, x_ss, x_rs, local_sem,
):
    s = lax.axis_index("segment")
    part = lax.axis_index("seq")
    z = lax.div(part, ROW)
    col = lax.rem(part, ROW)
    x = lax.div(col, C)
    c = lax.rem(col, C)
    after = lax.rem(s + 1, SECTIONS)
    before = lax.rem(s + SECTIONS - 1, SECTIONS)

    def in_row(section, d):
        return (section, z * ROW + lax.rem(col + d + ROW, ROW))

    def in_ring(d):
        return (s, lax.rem(z + d + Z, Z) * ROW + col)

    def along(d):
        return (s, lax.rem(part + d + PARTS, PARTS))

    barrier = pltpu.get_barrier_semaphore()
    greeted = (
        [in_row(before, -d) for d in range(ROW)]
        + [in_row(s, d) for d in range(1, ROW)]
        + [in_ring(d) for d in range(1, Z)]
        + [along(-2), along(-4)]
    )
    for device in greeted:
        pl.semaphore_signal(barrier, inc=1, device_id=device, device_id_type=MESH)
    keep = pltpu.make_async_copy(packed_ref, home_pk.at[x, z], local_sem.at[0])
    keep.start()
    fetch = pltpu.make_async_copy(fresh_ref, raw, local_sem.at[1])
    fetch.start()
    fetch_chosen = pltpu.make_async_copy(chosen_ref, chosen, local_sem.at[3])
    fetch_chosen.start()
    pl.semaphore_wait(barrier, len(greeted))

    pending = []

    def send(src, dst, send_sem, recv_sem, device):
        copy = pltpu.make_async_remote_copy(
            src_ref=src, dst_ref=dst, send_sem=send_sem, recv_sem=recv_sem,
            device_id=device, device_id_type=MESH,
        )
        copy.start()
        pending.append(copy)

    others = ((1, 0), (3, 0), (1, 1), (3, 1), (2, 0), (2, 1), (0, 1))

    def there(dx, dc):
        return lax.rem(x + dx + X, X) * C + lax.rem(c + dc, C)

    def arrived(ref, recv_sem):
        pltpu.make_async_remote_copy(
            src_ref=ref, dst_ref=ref, send_sem=recv_sem, recv_sem=recv_sem,
            device_id=in_ring(1), device_id_type=MESH,
        ).wait_recv()

    def piece_of(ref, i):
        return ref.at[pl.ds(PIECE * i, PIECE)]

    straight = (after, part)

    def send_cache(i):
        send(piece_of(cache_ref, i), piece_of(own, i), own_ss.at[i], own_rs.at[i], straight)

    def send_queries(i):
        send(q_ref.at[:, pl.ds(1024 * i, 1024)], qb.at[i], q_ss.at[i], q_rs.at[i], straight)

    def ring_send(k, i):
        for way, (held, sign) in enumerate(((right, 1), (left, -1))):
            if k < 4 or i // (CHUNKS // 2) == way:
                send(
                    piece_of(held[k - 1], i), piece_of(held[k], i),
                    ring_ss.at[way, k - 1, i], ring_rs.at[way, k - 1, i], in_ring(sign),
                )

    def ring_arrived(k, i):
        for way, held in enumerate((right, left)):
            if k < 4 or i // (CHUNKS // 2) == way:
                arrived(piece_of(held[k], i), ring_rs.at[way, k - 1, i])

    right = [own, r1, r2, r3, x4]
    left = [own, l1, l2, l3, x4]

    def serve(step, shard, d):
        owner = lax.rem(z + d + Z, Z) * ROW + col
        for e, (dx, dc) in enumerate(others + ((0, 0),)):
            peer = there(dx, dc)
            for r in range(2):
                block = shard[table[peer, r, owner]]
                if e == ROW - 1:
                    slots[owner, r] = block
                else:
                    stage[step, e, r] = block
            if e < ROW - 1:
                send(stage.at[step, e], slots.at[owner], x_ss.at[step, e], x_rs.at[step, e], (s, z * ROW + peer))

    def served(step, d):
        first = lax.rem(z + d + Z, Z) * ROW
        for e, (dx, dc) in enumerate(others):
            arrived(slots.at[first + there(-dx, dc)], x_rs.at[step, e])

    def gate(branch, head, rows):
        values = gate_of[rows, :]
        lane = lax.broadcasted_iota(jnp.int32, values.shape, 1)
        return jnp.sum(jnp.where(lane == branch * 32 + head, values, 0.0), axis=1, keepdims=True)

    def early_unit(i, u):
        g = i // 2
        q = jnp.concatenate(
            [qb[i, :, pl.ds(pl.multiple_of((2 * u + m) * HEAD, HEAD), HEAD)] for m in range(2)], axis=0
        )
        kv = pk[:, :, :, g].reshape(C * X * Z * 16, 2 * HEAD)
        scores = dot_nt(q, kv[:, :HEAD])
        peak = jnp.max(scores, axis=1, keepdims=True)
        weights = jnp.exp2((scores - peak) * EXP_SCALE).astype(jnp.bfloat16)
        mixed = dot_nn(weights, with_ones(kv[:, HEAD:]))
        summary = mixed[:, :HEAD] / mixed[:, HEAD:]

        near = fr[:, :, pl.ds(g * 2 * HEAD, 2 * HEAD)].reshape((REACH + 1) * TOKENS, 2 * HEAD)
        scores = dot_nt(q, near[:, :HEAD])
        key = lax.broadcasted_iota(jnp.int32, (2 * TOKENS, TOKENS), 1)
        token = lax.broadcasted_iota(jnp.int32, (2 * TOKENS, TOKENS), 0) & (TOKENS - 1)
        beyond = key > token
        piece = [scores[:, TOKENS * n : TOKENS * (n + 1)] for n in range(REACH + 1)]
        for n in range(REACH):
            piece[n] = jnp.where(key >= (REACH - n - part) * 1024, piece[n], MASKED)
        piece[0] = jnp.where(beyond, piece[0], piece[REACH])
        joined = jnp.concatenate(piece[:REACH], axis=1)
        peak = jnp.max(joined, axis=1, keepdims=True)
        weights = jnp.exp2((joined - peak) * EXP_SCALE)
        first = weights[:, :TOKENS]
        weights = jnp.concatenate(
            [jnp.where(beyond, first, 0.0), weights[:, TOKENS:], jnp.where(beyond, 0.0, first)], axis=1
        ).astype(jnp.bfloat16)
        mixed = dot_nn(weights, with_ones(near[:, HEAD:]))
        local = mixed[:, :HEAD] / mixed[:, HEAD:]

        for m in range(2):
            head = 8 * i + 2 * u + m
            rows = slice(TOKENS * m, TOKENS * (m + 1))
            everyone = slice(0, TOKENS)
            acc[8 * i + 2 * u + m] = (
                gate(0, head, everyone) * summary[rows] + gate(2, head, everyone) * local[rows]
            )

    def early(i, half):
        def body(u, carry):
            early_unit(i, u)
            return carry

        lax.fori_loop(2 * half, 2 * half + 2, body, 0)

    def late_unit(b, g, u):
        rows = slice(SPAN * b, SPAN * (b + 1))
        heads = [16 * g + 4 * u + m for m in range(4)]
        q = jnp.concatenate(
            [qb[h // 8, rows, (h % 8) * HEAD : (h % 8 + 1) * HEAD] for h in heads], axis=0
        )
        kv = sel[2 * b + g]
        scores = dot_nt(q, kv[:, :HEAD])
        peak = jnp.max(scores, axis=1, keepdims=True)
        weights = jnp.exp2((scores - peak) * EXP_SCALE).astype(jnp.bfloat16)
        mixed = dot_nn(weights, with_ones(kv[:, HEAD:]))
        picked = mixed[:, :HEAD] / mixed[:, HEAD:]
        for m, h in enumerate(heads):
            one = picked[SPAN * m : SPAN * (m + 1)]
            out_ref[rows, h * HEAD : (h + 1) * HEAD] = (
                acc[h, rows, :] + gate(1, h, rows) * one
            ).astype(jnp.bfloat16)

    sibling = (s, part + 1 - 2 * c)
    send_cache(0)
    for d in range(1, Z):
        send(packed_ref, home_pk.at[x, z], pk_ss.at[d], pk_rs.at[d], in_ring(d))
    fetch_chosen.wait()
    tile[...] = request_tile(chosen_row(chosen, listed))
    for d in range(ROW):
        send(tile, tiles.at[col], tile_ss.at[d], tile_rs.at[col], in_row(after, d))
    for i in range(1, CHUNKS):
        send_cache(i)
    fetch.wait()
    for g in range(KV_HEADS):
        behind[0, :, 2 * HEAD * g : 2 * HEAD * (g + 1)] = raw[:, g, :]
    send(behind.at[0], behind.at[1], misc_ss.at[2], misc_rs.at[2], along(2))
    send(behind.at[0], behind.at[2], misc_ss.at[3], misc_rs.at[3], along(4))
    for i in range(CHUNKS):
        arrived(piece_of(own, i), own_rs.at[i])
        ring_send(1, i)
        if i == 0:
            for d in range(ROW):
                arrived(tiles.at[d], tile_rs.at[d])
            to_scalar = pltpu.make_async_copy(tiles, table, local_sem.at[2])
            to_scalar.start()
        if i == 1:
            keep.wait()
            for d in range(1, Z):
                arrived(home_pk.at[x, lax.rem(z - d + Z, Z)], pk_rs.at[d])
            for d in range(1, X):
                to = (s, z * ROW + lax.rem(x + d, X) * C + c)
                send(home_pk.at[x], home_pk.at[x], pk_ss.at[Z + d], pk_rs.at[Z + d], to)
    to_scalar.wait()
    serve(0, own, 0)
    for d in range(1, X):
        arrived(home_pk.at[lax.rem(x - d + X, X)], pk_rs.at[Z + d])
    send(home_pk, pk.at[c], misc_ss.at[4], misc_rs.at[4], straight)
    arrived(behind.at[1], misc_rs.at[2])
    arrived(behind.at[2], misc_rs.at[3])
    for n, spot in enumerate((4, 2, 0)):
        send(behind.at[n], fr.at[spot], misc_ss.at[7 + n], misc_rs.at[7 + n], straight)
    send(gates_ref, gb, misc_ss.at[1], misc_rs.at[1], straight)
    send_queries(0)
    for i in range(CHUNKS):
        ring_arrived(1, i)
        ring_send(2, i)
    serve(1, r1, -1)
    serve(2, l1, 1)
    send_queries(1)
    for i in range(CHUNKS):
        ring_arrived(2, i)
        ring_send(3, i)
    serve(3, r2, -2)
    serve(4, l2, 2)
    send_queries(2)
    for i in range(CHUNKS):
        ring_arrived(3, i)
        ring_send(4, i)
        if i == 1:
            arrived(pk.at[c], misc_rs.at[4])
            send(pk.at[c], pk.at[c], misc_ss.at[10], misc_rs.at[10], sibling)
        if i == 2:
            for n, spot in enumerate((4, 2, 0)):
                arrived(fr.at[spot], misc_rs.at[7 + n])
            send(fr.at[4 - 2 * c], fr.at[3], misc_ss.at[5], misc_rs.at[5], sibling)
            send(fr.at[2 - 2 * c], fr.at[1], misc_ss.at[6], misc_rs.at[6], sibling)
    serve(5, r3, -3)
    serve(6, l3, 3)
    send_queries(3)
    arrived(gb, misc_rs.at[1])
    logits = jnp.concatenate([gb[...].astype(jnp.float32), jnp.zeros((32, TOKENS), jnp.float32)], axis=0)
    gate_of[...] = 1.0 / (1.0 + jnp.exp(-logits.T))
    arrived(pk.at[1 - c], misc_rs.at[10])
    arrived(fr.at[3], misc_rs.at[5])
    arrived(fr.at[1], misc_rs.at[6])
    arrived(qb.at[0], q_rs.at[0])
    early(0, 0)
    early(0, 1)
    for i in range(CHUNKS):
        ring_arrived(4, i)
    serve(7, x4, 4)
    for i in range(1, 4):
        arrived(qb.at[i], q_rs.at[i])
        early(i, 0)
        early(i, 1)
    for step, d in enumerate((0, -1, 1, -2, 2, -3, 3, 4)):
        served(step, d)
    for e in range(KV_HEADS * 2 * PICKED):
        spot = table[col, 2, e]
        sel[e // PICKED, pl.ds((e % PICKED) * SPAN, SPAN), :] = slots[lax.div(spot, 2), lax.rem(spot, 2)]
    for b in range(2):
        for g in range(KV_HEADS):
            for u in range(4):
                late_unit(b, g, u)
    for copy in pending:
        copy.wait_send()


def per_device(queries, cache, packed, fresh, gates, chosen):
    blocks = cache[0].reshape(KV_HEADS * 8, SPAN, 2 * HEAD)
    bf16, dma = jnp.bfloat16, pltpu.SemaphoreType.DMA
    shard = pltpu.VMEM((16, SPAN, 2 * HEAD), bf16)
    anywhere = pl.BlockSpec(memory_space=pltpu.HBM)
    vmem = pl.BlockSpec(memory_space=pltpu.VMEM)
    out = pl.pallas_call(
        kernel,
        out_shape=jax.ShapeDtypeStruct((TOKENS, WIDE), bf16),
        in_specs=[anywhere] * 6,
        out_specs=vmem,
        scratch_shapes=[shard] * 8
        + [
            pltpu.VMEM((8, ROW - 1, 2, SPAN, 2 * HEAD), bf16),
            pltpu.VMEM((PARTS, 2, SPAN, 2 * HEAD), bf16),
            pltpu.VMEM((X, Z, KV_HEADS, 16, 2 * HEAD), bf16),
            pltpu.VMEM((C, X, Z, KV_HEADS, 16, 2 * HEAD), bf16),
            pltpu.VMEM((TOKENS, KV_HEADS, 2 * HEAD), bf16),
            pltpu.VMEM((3, TOKENS, KV_HEADS * 2 * HEAD), bf16),
            pltpu.VMEM((REACH + 1, TOKENS, KV_HEADS * 2 * HEAD), bf16),
            pltpu.VMEM((4, TOKENS, 1024), bf16),
            pltpu.VMEM((96, TOKENS), bf16),
            pltpu.VMEM((TOKENS, 128), jnp.float32),
            pltpu.VMEM((2, KV_HEADS, PICKED), jnp.int32),
            pltpu.VMEM((8, 128), jnp.int32),
            pltpu.VMEM((8, 128), jnp.int32),
            pltpu.VMEM((ROW, 8, 128), jnp.int32),
            pltpu.VMEM((32, TOKENS, HEAD), jnp.float32),
            pltpu.VMEM((4, PICKED * SPAN, 2 * HEAD), bf16),
            pltpu.SMEM((ROW, 8, 128), jnp.int32),
            dma((ROW,)), dma((ROW,)),
            dma((Z + X,)), dma((Z + X,)),
            dma((CHUNKS,)), dma((CHUNKS,)),
            dma((11,)), dma((11,)),
            dma((4,)), dma((4,)),
            dma((2, 4, CHUNKS)), dma((2, 4, CHUNKS)),
            dma((8, ROW)), dma((8, ROW)),
            dma((4,)),
        ],
        compiler_params=pltpu.CompilerParams(
            collective_id=1, has_side_effects=True, vmem_limit_bytes=56 * 2**20
        ),
    )(queries[0], blocks, packed[0], fresh[0], gates[0].T, chosen[0])
    return out[None]


def solution(mesh):
    placed = (
        P("segment", "seq", None),
        P("segment", None, "seq", None),
        P("segment", None, "seq", None),
        P("segment", "seq", None, None),
        P("segment", "seq", None),
        P("segment", "seq", None, None),
    )
    return jax.shard_map(
        per_device, mesh=mesh, in_specs=placed, out_specs=P("segment", "seq", None), check_vma=False
    )
```

```python
import functools

import jax
import jax.numpy as jnp
from jax import lax
from jax.experimental import pallas as pl
from jax.experimental.pallas import tpu as pltpu
from jax.sharding import PartitionSpec as P

HEAD = 128
KV_HEADS = 2
GROUP = 16
SPAN = 64
PICKED = 16
TOKENS = 128
WIDE = KV_HEADS * GROUP * HEAD
Z, X, C = 8, 4, 2
ROW = X * C
PARTS = Z * ROW
SECTIONS = 4
REACH = 4
CHUNKS = 4
PIECE = KV_HEADS * 8 // CHUNKS
MESH = pl.DeviceIdType.MESH
MASKED = -1e30
EXP_SCALE = HEAD**-0.5 * 1.4426950408889634


def dot_nt(a, b):
    return lax.dot_general(a, b, (((1,), (1,)), ((), ())), preferred_element_type=jnp.float32)


def dot_nn(a, b):
    return lax.dot_general(a, b, (((1,), (0,)), ((), ())), preferred_element_type=jnp.float32)


def with_ones(v):
    return jnp.concatenate([v, jnp.ones(v.shape, v.dtype)], axis=1)


def request_tile(chosen_row):
    lane = lax.broadcasted_iota(jnp.int32, (128, 128), 1)
    down = lax.broadcasted_iota(jnp.int32, (128, 128), 0)
    across = jnp.broadcast_to(chosen_row, (128, 128))
    column = across.T
    owner_across = lax.shift_right_logical(across, 3)
    owner_down = lax.shift_right_logical(column, 3)
    head_down = lax.shift_right_logical(down, 4) & 1
    code_down = (column & 7) + 8 * head_down
    key_down = down * 16 + code_down
    mine = owner_down == lane
    first = jnp.min(jnp.where(mine, key_down, 1 << 16), axis=0, keepdims=True) & 15
    last = jnp.max(jnp.where(mine, key_down, 0), axis=0, keepdims=True) & 15
    earlier = (owner_down == owner_across) & (down < lane)
    rank = jnp.max(jnp.where(earlier, 1, 0), axis=0, keepdims=True)
    slot = owner_across[0:1] * 2 + rank
    pick = lax.broadcasted_iota(jnp.int32, (8, 128), 0)
    return jnp.where(pick == 0, first, jnp.where(pick == 1, last, slot))


def chosen_row(chosen_ref, listed):
    listed[...] = jnp.zeros(listed.shape, listed.dtype)
    for b in range(2):
        listed[KV_HEADS * b : KV_HEADS * (b + 1), 0:PICKED] = chosen_ref[b]
    lane = lax.broadcasted_iota(jnp.int32, (1, 128), 1)
    row = jnp.full((1, 128), 1 << 12, jnp.int32)
    for i in range(2 * KV_HEADS):
        part = listed[i : i + 1, :]
        if i > 0:
            part = pltpu.roll(part, PICKED * i, 1)
        row = jnp.where((lane >= PICKED * i) & (lane < PICKED * (i + 1)), part, row)
    return row


def kernel(
    q_ref, cache_ref, packed_ref, fresh_ref, gates_ref, chosen_ref, out_ref,
    own, r1, r2, r3, l1, l2, l3, x4, stage, slots, home_pk, pk, raw, behind, fr, qb, gb,
    gate_of, chosen, listed, tile, tiles, acc, sel, table,
    tile_ss, tile_rs, pk_ss, pk_rs, own_ss, own_rs, misc_ss, misc_rs, q_ss, q_rs,
    ring_ss, ring_rs, x_ss, x_rs, local_sem,
):
    s = lax.axis_index("segment")
    part = lax.axis_index("seq")
    z = lax.div(part, ROW)
    col = lax.rem(part, ROW)
    x = lax.div(col, C)
    c = lax.rem(col, C)
    after = lax.rem(s + 1, SECTIONS)
    before = lax.rem(s + SECTIONS - 1, SECTIONS)

    def in_row(section, d):
        return (section, z * ROW + lax.rem(col + d + ROW, ROW))

    def in_ring(d):
        return (s, lax.rem(z + d + Z, Z) * ROW + col)

    def along(d):
        return (s, lax.rem(part + d + PARTS, PARTS))

    barrier = pltpu.get_barrier_semaphore()
    greeted = (
        [in_row(before, -d) for d in range(ROW)]
        + [in_row(s, d) for d in range(1, ROW)]
        + [in_ring(d) for d in range(1, Z)]
        + [along(-2), along(-4)]
    )
    for device in greeted:
        pl.semaphore_signal(barrier, inc=1, device_id=device, device_id_type=MESH)
    keep = pltpu.make_async_copy(packed_ref, home_pk.at[x, z], local_sem.at[0])
    keep.start()
    fetch = pltpu.make_async_copy(fresh_ref, raw, local_sem.at[1])
    fetch.start()
    fetch_chosen = pltpu.make_async_copy(chosen_ref, chosen, local_sem.at[3])
    fetch_chosen.start()
    pl.semaphore_wait(barrier, len(greeted))

    pending = []

    def send(src, dst, send_sem, recv_sem, device):
        copy = pltpu.make_async_remote_copy(
            src_ref=src, dst_ref=dst, send_sem=send_sem, recv_sem=recv_sem,
            device_id=device, device_id_type=MESH,
        )
        copy.start()
        pending.append(copy)

    others = ((1, 0), (3, 0), (1, 1), (3, 1), (2, 0), (2, 1), (0, 1))

    def there(dx, dc):
        return lax.rem(x + dx + X, X) * C + lax.rem(c + dc, C)

    def arrived(ref, recv_sem):
        pltpu.make_async_remote_copy(
            src_ref=ref, dst_ref=ref, send_sem=recv_sem, recv_sem=recv_sem,
            device_id=in_ring(1), device_id_type=MESH,
        ).wait_recv()

    def piece_of(ref, i):
        return ref.at[pl.ds(PIECE * i, PIECE)]

    straight = (after, part)

    def send_cache(i):
        send(piece_of(cache_ref, i), piece_of(own, i), own_ss.at[i], own_rs.at[i], straight)

    def send_queries(i):
        send(q_ref.at[:, pl.ds(1024 * i, 1024)], qb.at[i], q_ss.at[i], q_rs.at[i], straight)

    def ring_send(k, i):
        for way, (held, sign) in enumerate(((right, 1), (left, -1))):
            if k < 4 or i // (CHUNKS // 2) == way:
                send(
                    piece_of(held[k - 1], i), piece_of(held[k], i),
                    ring_ss.at[way, k - 1, i], ring_rs.at[way, k - 1, i], in_ring(sign),
                )

    def ring_arrived(k, i):
        for way, held in enumerate((right, left)):
            if k < 4 or i // (CHUNKS // 2) == way:
                arrived(piece_of(held[k], i), ring_rs.at[way, k - 1, i])

    right = [own, r1, r2, r3, x4]
    left = [own, l1, l2, l3, x4]

    def serve(step, shard, d):
        owner = lax.rem(z + d + Z, Z) * ROW + col
        for e, (dx, dc) in enumerate(others + ((0, 0),)):
            peer = there(dx, dc)
            for r in range(2):
                block = shard[table[peer, r, owner]]
                if e == ROW - 1:
                    slots[owner, r] = block
                else:
                    stage[step, e, r] = block
            if e < ROW - 1:
                send(stage.at[step, e], slots.at[owner], x_ss.at[step, e], x_rs.at[step, e], (s, z * ROW + peer))

    def served(step, d):
        first = lax.rem(z + d + Z, Z) * ROW
        for e, (dx, dc) in enumerate(others):
            arrived(slots.at[first + there(-dx, dc)], x_rs.at[step, e])

    def gate(branch, head, rows):
        values = gate_of[rows, :]
        lane = lax.broadcasted_iota(jnp.int32, values.shape, 1)
        return jnp.sum(jnp.where(lane == branch * 32 + head, values, 0.0), axis=1, keepdims=True)

    def early_unit(i, u):
        g = i // 2
        q = jnp.concatenate(
            [qb[i, :, pl.ds(pl.multiple_of((2 * u + m) * HEAD, HEAD), HEAD)] for m in range(2)], axis=0
        )
        kv = pk[:, :, :, g].reshape(C * X * Z * 16, 2 * HEAD)
        scores = dot_nt(q, kv[:, :HEAD])
        peak = jnp.max(scores, axis=1, keepdims=True)
        weights = jnp.exp2((scores - peak) * EXP_SCALE).astype(jnp.bfloat16)
        mixed = dot_nn(weights, with_ones(kv[:, HEAD:]))
        summary = mixed[:, :HEAD] / mixed[:, HEAD:]

        near = fr[:, :, pl.ds(g * 2 * HEAD, 2 * HEAD)].reshape((REACH + 1) * TOKENS, 2 * HEAD)
        scores = dot_nt(q, near[:, :HEAD])
        key = lax.broadcasted_iota(jnp.int32, (2 * TOKENS, TOKENS), 1)
        token = lax.broadcasted_iota(jnp.int32, (2 * TOKENS, TOKENS), 0) & (TOKENS - 1)
        beyond = key > token
        piece = [scores[:, TOKENS * n : TOKENS * (n + 1)] for n in range(REACH + 1)]
        for n in range(REACH):
            piece[n] = jnp.where(key >= (REACH - n - part) * 1024, piece[n], MASKED)
        piece[0] = jnp.where(beyond, piece[0], piece[REACH])
        joined = jnp.concatenate(piece[:REACH], axis=1)
        peak = jnp.max(joined, axis=1, keepdims=True)
        weights = jnp.exp2((joined - peak) * EXP_SCALE)
        first = weights[:, :TOKENS]
        weights = jnp.concatenate(
            [jnp.where(beyond, first, 0.0), weights[:, TOKENS:], jnp.where(beyond, 0.0, first)], axis=1
        ).astype(jnp.bfloat16)
        mixed = dot_nn(weights, with_ones(near[:, HEAD:]))
        local = mixed[:, :HEAD] / mixed[:, HEAD:]

        for m in range(2):
            head = 8 * i + 2 * u + m
            rows = slice(TOKENS * m, TOKENS * (m + 1))
            everyone = slice(0, TOKENS)
            acc[8 * i + 2 * u + m] = (
                gate(0, head, everyone) * summary[rows] + gate(2, head, everyone) * local[rows]
            )

    def early(i, half):
        def body(u, carry):
            early_unit(i, u)
            return carry

        lax.fori_loop(2 * half, 2 * half + 2, body, 0)

    def late_unit(b, g, u):
        rows = slice(SPAN * b, SPAN * (b + 1))
        heads = [16 * g + 4 * u + m for m in range(4)]
        q = jnp.concatenate(
            [qb[h // 8, rows, (h % 8) * HEAD : (h % 8 + 1) * HEAD] for h in heads], axis=0
        )
        kv = sel[2 * b + g]
        scores = dot_nt(q, kv[:, :HEAD])
        peak = jnp.max(scores, axis=1, keepdims=True)
        weights = jnp.exp2((scores - peak) * EXP_SCALE).astype(jnp.bfloat16)
        mixed = dot_nn(weights, with_ones(kv[:, HEAD:]))
        picked = mixed[:, :HEAD] / mixed[:, HEAD:]
        for m, h in enumerate(heads):
            one = picked[SPAN * m : SPAN * (m + 1)]
            out_ref[rows, h * HEAD : (h + 1) * HEAD] = (
                acc[h, rows, :] + gate(1, h, rows) * one
            ).astype(jnp.bfloat16)

    sibling = (s, part + 1 - 2 * c)
    send_cache(0)
    send_cache(1)
    for d in range(1, Z):
        send(packed_ref, home_pk.at[x, z], pk_ss.at[d], pk_rs.at[d], in_ring(d))
    fetch_chosen.wait()
    tile[...] = request_tile(chosen_row(chosen, listed))
    for d in range(ROW):
        send(tile, tiles.at[col], tile_ss.at[d], tile_rs.at[col], in_row(after, d))
    for i in range(2, CHUNKS):
        send_cache(i)
    fetch.wait()
    for g in range(KV_HEADS):
        behind[0, :, 2 * HEAD * g : 2 * HEAD * (g + 1)] = raw[:, g, :]
    send(behind.at[0], behind.at[1], misc_ss.at[2], misc_rs.at[2], along(2))
    send(behind.at[0], behind.at[2], misc_ss.at[3], misc_rs.at[3], along(4))
    for i in range(CHUNKS):
        arrived(piece_of(own, i), own_rs.at[i])
        ring_send(1, i)
        if i == 2:
            for d in range(ROW):
                arrived(tiles.at[d], tile_rs.at[d])
            to_scalar = pltpu.make_async_copy(tiles, table, local_sem.at[2])
            to_scalar.start()
        if i == 1:
            keep.wait()
            for d in range(1, Z):
                arrived(home_pk.at[x, lax.rem(z - d + Z, Z)], pk_rs.at[d])
            for d in range(1, X):
                to = (s, z * ROW + lax.rem(x + d, X) * C + c)
                send(home_pk.at[x], home_pk.at[x], pk_ss.at[Z + d], pk_rs.at[Z + d], to)
    to_scalar.wait()
    serve(0, own, 0)
    for d in range(1, X):
        arrived(home_pk.at[lax.rem(x - d + X, X)], pk_rs.at[Z + d])
    send(home_pk, pk.at[c], misc_ss.at[4], misc_rs.at[4], straight)
    arrived(behind.at[1], misc_rs.at[2])
    arrived(behind.at[2], misc_rs.at[3])
    for n, spot in enumerate((4, 2, 0)):
        send(behind.at[n], fr.at[spot], misc_ss.at[7 + n], misc_rs.at[7 + n], straight)
    send(gates_ref, gb, misc_ss.at[1], misc_rs.at[1], straight)
    for i in range(4):
        send_queries(i)
    for i in range(CHUNKS):
        ring_arrived(1, i)
        ring_send(2, i)
    serve(1, r1, -1)
    serve(2, l1, 1)
    for i in range(CHUNKS):
        ring_arrived(2, i)
        ring_send(3, i)
    serve(3, r2, -2)
    serve(4, l2, 2)
    for i in range(CHUNKS):
        ring_arrived(3, i)
        ring_send(4, i)
        if i == 1:
            arrived(pk.at[c], misc_rs.at[4])
            send(pk.at[c], pk.at[c], misc_ss.at[10], misc_rs.at[10], sibling)
        if i == 2:
            for n, spot in enumerate((4, 2, 0)):
                arrived(fr.at[spot], misc_rs.at[7 + n])
            send(fr.at[4 - 2 * c], fr.at[3], misc_ss.at[5], misc_rs.at[5], sibling)
            send(fr.at[2 - 2 * c], fr.at[1], misc_ss.at[6], misc_rs.at[6], sibling)
    serve(5, r3, -3)
    serve(6, l3, 3)
    arrived(gb, misc_rs.at[1])
    logits = jnp.concatenate([gb[...].astype(jnp.float32), jnp.zeros((32, TOKENS), jnp.float32)], axis=0)
    gate_of[...] = 1.0 / (1.0 + jnp.exp(-logits.T))
    arrived(pk.at[1 - c], misc_rs.at[10])
    arrived(fr.at[3], misc_rs.at[5])
    arrived(fr.at[1], misc_rs.at[6])
    arrived(qb.at[0], q_rs.at[0])
    early(0, 0)
    early(0, 1)
    arrived(qb.at[1], q_rs.at[1])
    early(1, 0)
    for i in range(CHUNKS):
        ring_arrived(4, i)
    serve(7, x4, 4)
    early(1, 1)
    for i in range(2, 4):
        arrived(qb.at[i], q_rs.at[i])
        early(i, 0)
        early(i, 1)
    for step, d in enumerate((0, -1, 1, -2, 2, -3, 3, 4)):
        served(step, d)
    for e in range(KV_HEADS * 2 * PICKED):
        spot = table[col, 2, e]
        sel[e // PICKED, pl.ds((e % PICKED) * SPAN, SPAN), :] = slots[lax.div(spot, 2), lax.rem(spot, 2)]
    for b in range(2):
        for g in range(KV_HEADS):
            for u in range(4):
                late_unit(b, g, u)
    for copy in pending:
        copy.wait_send()


def per_device(queries, cache, packed, fresh, gates, chosen):
    blocks = cache[0].reshape(KV_HEADS * 8, SPAN, 2 * HEAD)
    bf16, dma = jnp.bfloat16, pltpu.SemaphoreType.DMA
    shard = pltpu.VMEM((16, SPAN, 2 * HEAD), bf16)
    anywhere = pl.BlockSpec(memory_space=pltpu.HBM)
    vmem = pl.BlockSpec(memory_space=pltpu.VMEM)
    operands = queries[0], blocks, packed[0], fresh[0], gates[0].T, chosen[0]
    out = pl.pallas_call(
        kernel,
        out_shape=jax.ShapeDtypeStruct((TOKENS, WIDE), bf16),
        in_specs=[anywhere] * 6,
        out_specs=vmem,
        scratch_shapes=[shard] * 8
        + [
            pltpu.VMEM((8, ROW - 1, 2, SPAN, 2 * HEAD), bf16),
            pltpu.VMEM((PARTS, 2, SPAN, 2 * HEAD), bf16),
            pltpu.VMEM((X, Z, KV_HEADS, 16, 2 * HEAD), bf16),
            pltpu.VMEM((C, X, Z, KV_HEADS, 16, 2 * HEAD), bf16),
            pltpu.VMEM((TOKENS, KV_HEADS, 2 * HEAD), bf16),
            pltpu.VMEM((3, TOKENS, KV_HEADS * 2 * HEAD), bf16),
            pltpu.VMEM((REACH + 1, TOKENS, KV_HEADS * 2 * HEAD), bf16),
            pltpu.VMEM((4, TOKENS, 1024), bf16),
            pltpu.VMEM((96, TOKENS), bf16),
            pltpu.VMEM((TOKENS, 128), jnp.float32),
            pltpu.VMEM((2, KV_HEADS, PICKED), jnp.int32),
            pltpu.VMEM((8, 128), jnp.int32),
            pltpu.VMEM((8, 128), jnp.int32),
            pltpu.VMEM((ROW, 8, 128), jnp.int32),
            pltpu.VMEM((32, TOKENS, HEAD), jnp.float32),
            pltpu.VMEM((4, PICKED * SPAN, 2 * HEAD), bf16),
            pltpu.SMEM((ROW, 8, 128), jnp.int32),
            dma((ROW,)), dma((ROW,)),
            dma((Z + X,)), dma((Z + X,)),
            dma((CHUNKS,)), dma((CHUNKS,)),
            dma((11,)), dma((11,)),
            dma((4,)), dma((4,)),
            dma((2, 4, CHUNKS)), dma((2, 4, CHUNKS)),
            dma((8, ROW)), dma((8, ROW)),
            dma((4,)),
        ],
        compiler_params=pltpu.CompilerParams(
            collective_id=1, has_side_effects=True, vmem_limit_bytes=48 * 2**20
        ),
    )(*(pltpu.with_memory_space_constraint(operand, pltpu.HBM) for operand in operands))
    return out[None]


def solution(mesh):
    placed = (
        P("segment", "seq", None),
        P("segment", None, "seq", None),
        P("segment", None, "seq", None),
        P("segment", "seq", None, None),
        P("segment", "seq", None),
        P("segment", "seq", None, None),
    )
    return jax.shard_map(
        per_device, mesh=mesh, in_specs=placed, out_specs=P("segment", "seq", None), check_vma=False
    )
```

```python
import functools

import jax
import jax.numpy as jnp
from jax import lax
from jax.experimental import pallas as pl
from jax.experimental.pallas import tpu as pltpu
from jax.sharding import PartitionSpec as P

HEAD = 128
KV_HEADS = 2
GROUP = 16
SPAN = 64
PICKED = 16
TOKENS = 128
WIDE = KV_HEADS * GROUP * HEAD
Z, X, C = 8, 4, 2
ROW = X * C
PARTS = Z * ROW
SECTIONS = 4
REACH = 4
CHUNKS = 4
PIECE = KV_HEADS * 8 // CHUNKS
MESH = pl.DeviceIdType.MESH
MASKED = -1e30
EXP_SCALE = HEAD**-0.5 * 1.4426950408889634


def dot_nt(a, b):
    return lax.dot_general(a, b, (((1,), (1,)), ((), ())), preferred_element_type=jnp.float32)


def dot_nn(a, b):
    return lax.dot_general(a, b, (((1,), (0,)), ((), ())), preferred_element_type=jnp.float32)


def with_ones(v):
    return jnp.concatenate([v, jnp.ones(v.shape, v.dtype)], axis=1)


def request_tile(chosen_row):
    lane = lax.broadcasted_iota(jnp.int32, (128, 128), 1)
    down = lax.broadcasted_iota(jnp.int32, (128, 128), 0)
    across = jnp.broadcast_to(chosen_row, (128, 128))
    column = across.T
    owner_across = lax.shift_right_logical(across, 3)
    owner_down = lax.shift_right_logical(column, 3)
    head_down = lax.shift_right_logical(down, 4) & 1
    code_down = (column & 7) + 8 * head_down
    key_down = down * 16 + code_down
    mine = owner_down == lane
    first = jnp.min(jnp.where(mine, key_down, 1 << 16), axis=0, keepdims=True) & 15
    last = jnp.max(jnp.where(mine, key_down, 0), axis=0, keepdims=True) & 15
    earlier = (owner_down == owner_across) & (down < lane)
    rank = jnp.max(jnp.where(earlier, 1, 0), axis=0, keepdims=True)
    slot = owner_across[0:1] * 2 + rank
    pick = lax.broadcasted_iota(jnp.int32, (8, 128), 0)
    return jnp.where(pick == 0, first, jnp.where(pick == 1, last, slot))


def chosen_row(chosen_ref, listed):
    listed[...] = jnp.zeros(listed.shape, listed.dtype)
    for b in range(2):
        listed[KV_HEADS * b : KV_HEADS * (b + 1), 0:PICKED] = chosen_ref[b]
    lane = lax.broadcasted_iota(jnp.int32, (1, 128), 1)
    row = jnp.full((1, 128), 1 << 12, jnp.int32)
    for i in range(2 * KV_HEADS):
        part = listed[i : i + 1, :]
        if i > 0:
            part = pltpu.roll(part, PICKED * i, 1)
        row = jnp.where((lane >= PICKED * i) & (lane < PICKED * (i + 1)), part, row)
    return row


def kernel(
    q_ref, cache_ref, packed_ref, fresh_ref, gates_ref, chosen_ref, out_ref,
    own, r1, r2, r3, l1, l2, l3, x4, stage, slots, home_pk, pk, raw, behind, fr, qb, gb,
    gate_of, chosen, listed, tile, tiles, acc, sel, table,
    tile_ss, tile_rs, pk_ss, pk_rs, own_ss, own_rs, misc_ss, misc_rs, q_ss, q_rs,
    ring_ss, ring_rs, x_ss, x_rs, local_sem,
):
    s = lax.axis_index("segment")
    part = lax.axis_index("seq")
    z = lax.div(part, ROW)
    col = lax.rem(part, ROW)
    x = lax.div(col, C)
    c = lax.rem(col, C)
    after = lax.rem(s + 1, SECTIONS)
    before = lax.rem(s + SECTIONS - 1, SECTIONS)

    def in_row(section, d):
        return (section, z * ROW + lax.rem(col + d + ROW, ROW))

    def in_ring(d):
        return (s, lax.rem(z + d + Z, Z) * ROW + col)

    def along(d):
        return (s, lax.rem(part + d + PARTS, PARTS))

    barrier = pltpu.get_barrier_semaphore()
    greeted = (
        [in_row(before, -d) for d in range(ROW)]
        + [in_row(s, d) for d in range(1, ROW)]
        + [in_ring(d) for d in range(1, Z)]
        + [along(-2), along(-4)]
    )
    for device in greeted:
        pl.semaphore_signal(barrier, inc=1, device_id=device, device_id_type=MESH)
    keep = pltpu.make_async_copy(packed_ref, home_pk.at[x, z], local_sem.at[0])
    keep.start()
    fetch = pltpu.make_async_copy(fresh_ref, raw, local_sem.at[1])
    fetch.start()
    fetch_chosen = pltpu.make_async_copy(chosen_ref, chosen, local_sem.at[3])
    fetch_chosen.start()
    pl.semaphore_wait(barrier, len(greeted))

    pending = []

    def send(src, dst, send_sem, recv_sem, device):
        copy = pltpu.make_async_remote_copy(
            src_ref=src, dst_ref=dst, send_sem=send_sem, recv_sem=recv_sem,
            device_id=device, device_id_type=MESH,
        )
        copy.start()
        pending.append(copy)

    others = ((2, 0), (1, 0), (3, 0), (2, 1), (1, 1), (3, 1), (0, 1))

    def there(dx, dc):
        return lax.rem(x + dx + X, X) * C + lax.rem(c + dc, C)

    def arrived(ref, recv_sem):
        pltpu.make_async_remote_copy(
            src_ref=ref, dst_ref=ref, send_sem=recv_sem, recv_sem=recv_sem,
            device_id=in_ring(1), device_id_type=MESH,
        ).wait_recv()

    def piece_of(ref, i):
        return ref.at[pl.ds(PIECE * i, PIECE)]

    straight = (after, part)

    def send_cache(i):
        send(piece_of(cache_ref, i), piece_of(own, i), own_ss.at[i], own_rs.at[i], straight)

    def send_queries(i):
        send(q_ref.at[:, pl.ds(1024 * i, 1024)], qb.at[i], q_ss.at[i], q_rs.at[i], straight)

    def ring_send(k, i):
        for way, (held, sign) in enumerate(((right, 1), (left, -1))):
            if k < 4 or i // (CHUNKS // 2) == way:
                send(
                    piece_of(held[k - 1], i), piece_of(held[k], i),
                    ring_ss.at[way, k - 1, i], ring_rs.at[way, k - 1, i], in_ring(sign),
                )

    def ring_arrived(k, i):
        for way, held in enumerate((right, left)):
            if k < 4 or i // (CHUNKS // 2) == way:
                arrived(piece_of(held[k], i), ring_rs.at[way, k - 1, i])

    right = [own, r1, r2, r3, x4]
    left = [own, l1, l2, l3, x4]

    def serve(step, shard, d):
        owner = lax.rem(z + d + Z, Z) * ROW + col
        for e, (dx, dc) in enumerate(others + ((0, 0),)):
            peer = there(dx, dc)
            for r in range(2):
                block = shard[table[peer, r, owner]]
                if e == ROW - 1:
                    slots[owner, r] = block
                else:
                    stage[step, e, r] = block
            if e < ROW - 1:
                send(stage.at[step, e], slots.at[owner], x_ss.at[step, e], x_rs.at[step, e], (s, z * ROW + peer))

    def served(step, d):
        first = lax.rem(z + d + Z, Z) * ROW
        for e, (dx, dc) in enumerate(others):
            arrived(slots.at[first + there(-dx, dc)], x_rs.at[step, e])

    def gate(branch, head, rows):
        values = gate_of[rows, :]
        lane = lax.broadcasted_iota(jnp.int32, values.shape, 1)
        return jnp.sum(jnp.where(lane == branch * 32 + head, values, 0.0), axis=1, keepdims=True)

    def early_unit(i, u):
        g = i // 2
        q = jnp.concatenate(
            [qb[i, :, pl.ds((2 * u + m) * HEAD, HEAD)] for m in range(2)], axis=0
        )
        kv = pk[:, :, :, g].reshape(C * X * Z * 16, 2 * HEAD)
        scores = dot_nt(q, kv[:, :HEAD])
        peak = jnp.max(scores, axis=1, keepdims=True)
        weights = jnp.exp2((scores - peak) * EXP_SCALE).astype(jnp.bfloat16)
        mixed = dot_nn(weights, with_ones(kv[:, HEAD:]))
        summary = mixed[:, :HEAD] / mixed[:, HEAD:]

        near = fr[:, :, pl.ds(g * 2 * HEAD, 2 * HEAD)].reshape((REACH + 1) * TOKENS, 2 * HEAD)
        scores = dot_nt(q, near[:, :HEAD])
        key = lax.broadcasted_iota(jnp.int32, (2 * TOKENS, TOKENS), 1)
        token = lax.broadcasted_iota(jnp.int32, (2 * TOKENS, TOKENS), 0) & (TOKENS - 1)
        beyond = key > token
        piece = [scores[:, TOKENS * n : TOKENS * (n + 1)] for n in range(REACH + 1)]
        for n in range(REACH):
            piece[n] = jnp.where(key >= (REACH - n - part) * 1024, piece[n], MASKED)
        piece[0] = jnp.where(beyond, piece[0], piece[REACH])
        joined = jnp.concatenate(piece[:REACH], axis=1)
        peak = jnp.max(joined, axis=1, keepdims=True)
        weights = jnp.exp2((joined - peak) * EXP_SCALE)
        first = weights[:, :TOKENS]
        weights = jnp.concatenate(
            [jnp.where(beyond, first, 0.0), weights[:, TOKENS:], jnp.where(beyond, 0.0, first)], axis=1
        ).astype(jnp.bfloat16)
        mixed = dot_nn(weights, with_ones(near[:, HEAD:]))
        local = mixed[:, :HEAD] / mixed[:, HEAD:]

        for m in range(2):
            head = 8 * i + 2 * u + m
            rows = slice(TOKENS * m, TOKENS * (m + 1))
            everyone = slice(0, TOKENS)
            acc[8 * i + 2 * u + m] = (
                gate(0, head, everyone) * summary[rows] + gate(2, head, everyone) * local[rows]
            )

    def early(i, half):
        early_unit(i, 2 * half)
        early_unit(i, 2 * half + 1)

    def late_unit(b, g, u):
        rows = slice(SPAN * b, SPAN * (b + 1))
        heads = [16 * g + 4 * u + m for m in range(4)]
        q = jnp.concatenate(
            [qb[h // 8, rows, (h % 8) * HEAD : (h % 8 + 1) * HEAD] for h in heads], axis=0
        )
        kv = sel[2 * b + g]
        scores = dot_nt(q, kv[:, :HEAD])
        peak = jnp.max(scores, axis=1, keepdims=True)
        weights = jnp.exp2((scores - peak) * EXP_SCALE).astype(jnp.bfloat16)
        mixed = dot_nn(weights, with_ones(kv[:, HEAD:]))
        picked = mixed[:, :HEAD] / mixed[:, HEAD:]
        for m, h in enumerate(heads):
            one = picked[SPAN * m : SPAN * (m + 1)]
            out_ref[rows, h * HEAD : (h + 1) * HEAD] = (
                acc[h, rows, :] + gate(1, h, rows) * one
            ).astype(jnp.bfloat16)

    sibling = (s, part + 1 - 2 * c)
    send_cache(0)
    send_cache(1)
    for d in range(1, Z):
        send(packed_ref, home_pk.at[x, z], pk_ss.at[d], pk_rs.at[d], in_ring(d))
    fetch_chosen.wait()
    tile[...] = request_tile(chosen_row(chosen, listed))
    for d in range(ROW):
        send(tile, tiles.at[col], tile_ss.at[d], tile_rs.at[col], in_row(after, d))
    for i in range(2, CHUNKS):
        send_cache(i)
    fetch.wait()
    for g in range(KV_HEADS):
        behind[0, :, 2 * HEAD * g : 2 * HEAD * (g + 1)] = raw[:, g, :]
    send(behind.at[0], behind.at[1], misc_ss.at[2], misc_rs.at[2], along(2))
    send(behind.at[0], behind.at[2], misc_ss.at[3], misc_rs.at[3], along(4))
    for i in range(CHUNKS):
        arrived(piece_of(own, i), own_rs.at[i])
        ring_send(1, i)
        if i == 2:
            for d in range(ROW):
                arrived(tiles.at[d], tile_rs.at[d])
            to_scalar = pltpu.make_async_copy(tiles, table, local_sem.at[2])
            to_scalar.start()
        if i == 1:
            keep.wait()
            for d in range(1, Z):
                arrived(home_pk.at[x, lax.rem(z - d + Z, Z)], pk_rs.at[d])
            for d in range(1, X):
                to = (s, z * ROW + lax.rem(x + d, X) * C + c)
                send(home_pk.at[x], home_pk.at[x], pk_ss.at[Z + d], pk_rs.at[Z + d], to)
    to_scalar.wait()
    serve(0, own, 0)
    for d in range(1, X):
        arrived(home_pk.at[lax.rem(x - d + X, X)], pk_rs.at[Z + d])
    send(home_pk, pk.at[c], misc_ss.at[4], misc_rs.at[4], straight)
    arrived(behind.at[1], misc_rs.at[2])
    arrived(behind.at[2], misc_rs.at[3])
    for n, spot in enumerate((4, 2, 0)):
        send(behind.at[n], fr.at[spot], misc_ss.at[7 + n], misc_rs.at[7 + n], straight)
    send(gates_ref, gb, misc_ss.at[1], misc_rs.at[1], straight)
    for i in range(4):
        send_queries(i)
    for i in range(CHUNKS):
        ring_arrived(1, i)
        ring_send(2, i)
    serve(1, r1, -1)
    serve(2, l1, 1)
    for i in range(CHUNKS):
        ring_arrived(2, i)
        ring_send(3, i)
    serve(3, r2, -2)
    serve(4, l2, 2)
    for i in range(CHUNKS):
        ring_arrived(3, i)
        ring_send(4, i)
        if i == 1:
            arrived(pk.at[c], misc_rs.at[4])
            send(pk.at[c], pk.at[c], misc_ss.at[10], misc_rs.at[10], sibling)
        if i == 2:
            for n, spot in enumerate((4, 2, 0)):
                arrived(fr.at[spot], misc_rs.at[7 + n])
            send(fr.at[4 - 2 * c], fr.at[3], misc_ss.at[5], misc_rs.at[5], sibling)
            send(fr.at[2 - 2 * c], fr.at[1], misc_ss.at[6], misc_rs.at[6], sibling)
    serve(5, r3, -3)
    serve(6, l3, 3)
    arrived(gb, misc_rs.at[1])
    logits = jnp.concatenate([gb[...].astype(jnp.float32), jnp.zeros((32, TOKENS), jnp.float32)], axis=0)
    gate_of[...] = 1.0 / (1.0 + jnp.exp(-logits.T))
    arrived(pk.at[1 - c], misc_rs.at[10])
    arrived(fr.at[3], misc_rs.at[5])
    arrived(fr.at[1], misc_rs.at[6])
    arrived(qb.at[0], q_rs.at[0])
    early(0, 0)
    early(0, 1)
    arrived(qb.at[1], q_rs.at[1])
    early(1, 0)
    for i in range(CHUNKS):
        ring_arrived(4, i)
    serve(7, x4, 4)
    early(1, 1)
    for i in range(2, 4):
        arrived(qb.at[i], q_rs.at[i])
        early(i, 0)
        early(i, 1)
    for step, d in enumerate((0, -1, 1, -2, 2, -3, 3, 4)):
        served(step, d)
    for e in range(KV_HEADS * 2 * PICKED):
        spot = table[col, 2, e]
        sel[e // PICKED, pl.ds((e % PICKED) * SPAN, SPAN), :] = slots[lax.div(spot, 2), lax.rem(spot, 2)]
    for b in range(2):
        for g in range(KV_HEADS):
            for u in range(4):
                late_unit(b, g, u)
    for copy in pending:
        copy.wait_send()


def per_device(queries, cache, packed, fresh, gates, chosen):
    blocks = cache[0].reshape(KV_HEADS * 8, SPAN, 2 * HEAD)
    bf16, dma = jnp.bfloat16, pltpu.SemaphoreType.DMA
    shard = pltpu.VMEM((16, SPAN, 2 * HEAD), bf16)
    anywhere = pl.BlockSpec(memory_space=pltpu.HBM)
    vmem = pl.BlockSpec(memory_space=pltpu.VMEM)
    operands = queries[0], blocks, packed[0], fresh[0], gates[0].T, chosen[0]
    out = pl.pallas_call(
        kernel,
        out_shape=jax.ShapeDtypeStruct((TOKENS, WIDE), bf16),
        in_specs=[anywhere] * 6,
        out_specs=vmem,
        scratch_shapes=[shard] * 8
        + [
            pltpu.VMEM((8, ROW - 1, 2, SPAN, 2 * HEAD), bf16),
            pltpu.VMEM((PARTS, 2, SPAN, 2 * HEAD), bf16),
            pltpu.VMEM((X, Z, KV_HEADS, 16, 2 * HEAD), bf16),
            pltpu.VMEM((C, X, Z, KV_HEADS, 16, 2 * HEAD), bf16),
            pltpu.VMEM((TOKENS, KV_HEADS, 2 * HEAD), bf16),
            pltpu.VMEM((3, TOKENS, KV_HEADS * 2 * HEAD), bf16),
            pltpu.VMEM((REACH + 1, TOKENS, KV_HEADS * 2 * HEAD), bf16),
            pltpu.VMEM((4, TOKENS, 1024), bf16),
            pltpu.VMEM((96, TOKENS), bf16),
            pltpu.VMEM((TOKENS, 128), jnp.float32),
            pltpu.VMEM((2, KV_HEADS, PICKED), jnp.int32),
            pltpu.VMEM((8, 128), jnp.int32),
            pltpu.VMEM((8, 128), jnp.int32),
            pltpu.VMEM((ROW, 8, 128), jnp.int32),
            pltpu.VMEM((32, TOKENS, HEAD), jnp.float32),
            pltpu.VMEM((4, PICKED * SPAN, 2 * HEAD), bf16),
            pltpu.SMEM((ROW, 8, 128), jnp.int32),
            dma((ROW,)), dma((ROW,)),
            dma((Z + X,)), dma((Z + X,)),
            dma((CHUNKS,)), dma((CHUNKS,)),
            dma((11,)), dma((11,)),
            dma((4,)), dma((4,)),
            dma((2, 4, CHUNKS)), dma((2, 4, CHUNKS)),
            dma((8, ROW)), dma((8, ROW)),
            dma((4,)),
        ],
        compiler_params=pltpu.CompilerParams(
            collective_id=1, has_side_effects=True, vmem_limit_bytes=48 * 2**20
        ),
    )(*(pltpu.with_memory_space_constraint(operand, pltpu.HBM) for operand in operands))
    return out[None]


def solution(mesh):
    placed = (
        P("segment", "seq", None),
        P("segment", None, "seq", None),
        P("segment", None, "seq", None),
        P("segment", "seq", None, None),
        P("segment", "seq", None),
        P("segment", "seq", None, None),
    )
    return jax.shard_map(
        per_device, mesh=mesh, in_specs=placed, out_specs=P("segment", "seq", None), check_vma=False
    )
```
